32 devices in a mesh: dp: 8 (over y, x, core), seq: 4 (over z).
Axes of the slice: x: 2, y: 2, z: 4, core: 2. Of those that a mesh axis runs over, the one named last changes fastest.
Arguments:
- audio_blocks: bfloat16 [8, 64, 320], P('dp', 'seq'), may hold values from -6 to 6
- send_list: int32 [4, 8, 32], P('seq', 'dp'), may hold values from -1 to 15, as said below
- place_list: int32 [4, 8, 16], P('seq', 'dp'), may hold values from 0 to 31, as said below
- cotangent: bfloat16 [8, 2048, 512], P('dp', 'seq'), may hold values from -0.046875 to 0.046875
- conv_zero: bfloat16 [10, 512], replicated, may hold values from -2 to 2
- conv_one: bfloat16 [1536, 512], replicated, may hold values from -0.15625 to 0.15625
- gain_zero: float32 [512], replicated, may hold values from 0.25 to 1.75
- bias_zero: float32 [512], replicated, may hold values from -3 to 3
- gain_one: float32 [512], replicated, may hold values from 0.25 to 1.75
- bias_one: float32 [512], replicated, may hold values from -3 to 3
Outputs:
- features: bfloat16 [8, 2048, 512], P('dp', 'seq')
- grad_conv_one: float32 [1536, 512], P('dp')
- grad_conv_zero: float32 [10, 512], replicated
- grad_gain_zero: float32 [512], replicated
- grad_bias_zero: float32 [512], replicated
- grad_gain_one: float32 [512], replicated
- grad_bias_one: float32 [512], replicated
The draws below stay inside these ranges and needn't reach their ends.
Inputs may be any that keep to these rules, and one draw needn't show every extreme that they name: `send_list`: row (s, i) holds, in 4 slots for each destination device in order, the local blocks of store s on device i sent there; -1 marks an empty slot. Each of the 16 blocks appears exactly once in its row, and in every store some source fills all 4 slots to some destination. `place_list`: row (s, j) names 16 distinct filled received slots (source times 4 plus slot) for device j and store s, in the order of its segment.
All inputs are finite; a program needn't handle non-finite values.
Results may differ from the reference program's by a relative error of at most 0.0057.
Values may be sent and summed in bfloat16 or wider, within the bound.
No kernel may reach another device: no remote copies, remote signals or barrier semaphores. Data moves between devices by JAX's collectives and lax.ppermute only.
A program may use at most 64 MiB of HBM per device.

```python
import jax
import jax.numpy as jnp
from jax import lax

C = 512
FR1 = 512
CAP = 4
ROWS = 16
BLEN = 320
N_DP = 8
N_SEQ = 4


def store_lists(key):
    subkeys = jax.random.split(key, 5)
    half_count = N_DP // 2
    tilted = jax.random.randint(subkeys[0], (half_count, half_count), -2, 3)
    tilted = tilted.at[0, 0].set(2)
    upper_half = jnp.stack([2 + tilted, 2 - tilted], axis=-1)
    lower_half = jnp.stack([2 - tilted, 2 + tilted], axis=-1)
    counts = jnp.stack([upper_half, lower_half], axis=1).reshape(N_DP, N_DP)
    counts = counts[jax.random.permutation(subkeys[1], N_DP)][:, jax.random.permutation(subkeys[2], N_DP)]
    orders = jax.vmap(lambda subkey: jax.random.permutation(subkey, ROWS))(jax.random.split(subkeys[3], N_DP))
    starts = jnp.cumsum(counts, axis=1) - counts
    slot_ids = jnp.arange(CAP)
    wanted = starts[:, :, None] + slot_ids
    filled = slot_ids < counts[:, :, None]
    local_ids = jnp.take_along_axis(orders, jnp.clip(wanted, 0, ROWS - 1).reshape(N_DP, N_DP * CAP), axis=1)
    send_lists = jnp.where(filled.reshape(N_DP, N_DP * CAP), local_ids, -1)
    arrived = jnp.transpose(filled, (1, 0, 2)).reshape(N_DP, N_DP * CAP)
    rank_ids = jax.vmap(lambda subkey: jax.random.permutation(subkey, N_DP * CAP))(jax.random.split(subkeys[4], N_DP))
    scores = jnp.where(arrived, rank_ids, rank_ids + N_DP * CAP)
    places = jnp.argsort(scores, axis=1)[:, :ROWS]
    return (send_lists.astype(jnp.int32), places.astype(jnp.int32))


def reassign_lists(key):
    base_key = jax.random.fold_in(key, 31)
    return jax.vmap(store_lists)(jax.random.split(base_key, N_SEQ))


def draw_send_list(key, part):
    return reassign_lists(key)[0]


def draw_place_list(key, part):
    return reassign_lists(key)[1]


def steps_of(key, dims, cuts, smallest, top_value):
    def one(position, blocks):
        steps = jax.random.uniform(jax.random.fold_in(jax.random.fold_in(key, 6), position), (blocks,), jnp.float32, smallest / len(cuts), top_value / len(cuts))
        return jnp.repeat(jnp.exp(steps), dims[position] // blocks).reshape((-1,) + (1,) * (len(dims) - position - 1))

    loudness = one(*cuts[0])
    for cut in cuts[1:]:
        loudness = loudness * one(*cut)
    return loudness


def scatter_about(rng, shape, scale, reach, cuts=(), held_as=jnp.bfloat16):
    values = scale * jax.random.normal(rng, shape, jnp.float32)
    if cuts:
        values = values * steps_of(rng, shape, cuts, -0.22, 0.18)
    return jnp.clip(values, -reach, reach).astype(held_as)


def setup_inputs(seed: int = 0) -> dict:
    streams_of = jax.random.split(jax.random.key(seed), 11)
    return {
        "audio_blocks": scatter_about(streams_of[0], (N_DP, N_SEQ * ROWS, BLEN), 1.0, 6.0, ((0, 8), (1, 4))),
        "send_list": draw_send_list(jax.random.fold_in(streams_of[10], 71), 0),
        "place_list": draw_place_list(jax.random.fold_in(streams_of[10], 71), 0),
        "cotangent": scatter_about(streams_of[3], (N_DP, N_SEQ * FR1, C), (N_DP * N_SEQ * FR1) ** -0.5, 0.046875, ((0, 8), (1, 4))),
        "conv_zero": scatter_about(streams_of[4], (10, C), 10 ** -0.5, 2.0),
        "conv_one": scatter_about(streams_of[5], (3 * C, C), (3 * C) ** -0.5, 0.15625),
        "gain_zero": jnp.clip(1.0 + 0.15 * jax.random.normal(streams_of[6], (C,), jnp.float32), 0.25, 1.75),
        "bias_zero": scatter_about(streams_of[7], (C,), 0.5, 3.0, (), jnp.float32),
        "gain_one": jnp.clip(1.0 + 0.15 * jax.random.normal(streams_of[8], (C,), jnp.float32), 0.25, 1.75),
        "bias_one": scatter_about(streams_of[9], (C,), 0.5, 3.0, (), jnp.float32),
    }


norm_eps = 1e-05

def gelu_slope(argument):
    return 0.5 * (1.0 + lax.erf(argument * 0.7071067811865476)) + argument * jnp.exp(-0.5 * argument * argument) * 0.3989422804014327

def norm_forward(pre_act, gain_vec, bias_vec):
    center = pre_act - lax.optimization_barrier(jnp.mean(pre_act, axis=-1, keepdims=True))
    spread = lax.rsqrt(lax.optimization_barrier(jnp.mean(center * center, axis=-1, keepdims=True)) + norm_eps)
    scaled = center * spread
    normed = scaled * gain_vec + bias_vec
    return (jax.nn.gelu(normed, approximate=False), scaled, spread, normed)

def norm_backward(upstream, gain_vec, scaled, spread, normed):
    inner_grad = upstream * gelu_slope(normed)
    grad_gain = lax.optimization_barrier(jnp.sum(inner_grad * scaled, axis=0))
    grad_bias = lax.optimization_barrier(jnp.sum(inner_grad, axis=0))
    pushed = inner_grad * gain_vec
    back_grad = spread * (pushed - lax.optimization_barrier(jnp.mean(pushed, axis=-1, keepdims=True)) - scaled * lax.optimization_barrier(jnp.mean(pushed * scaled, axis=-1, keepdims=True)))
    return (back_grad, grad_gain, grad_bias)

def frame_patches(samples, frames):
    sample_rows = samples[:5 * (frames + 1)].reshape(frames + 1, 5)
    return jnp.concatenate([sample_rows[:-1], sample_rows[1:]], axis=1)

def layer_one(frames_in, frames_one, conv_one, gain_one, bias_one, upstream):
    width = conv_one.shape[1]
    frame_pairs = frames_in[:2 * frames_one].reshape(frames_one, 2, width)
    first_tap = frame_pairs[:, 0]
    second_tap = frame_pairs[:, 1]
    third_tap = jnp.concatenate([first_tap[1:], frames_in[2 * frames_one:]], axis=0)
    pre_one = jnp.dot(first_tap, conv_one[:width], preferred_element_type=jnp.float32) + jnp.dot(second_tap, conv_one[width:2 * width], preferred_element_type=jnp.float32) + jnp.dot(third_tap, conv_one[2 * width:], preferred_element_type=jnp.float32)
    act_one, scaled_one, spread_one, normed_one = norm_forward(pre_one, gain_one, bias_one)
    back_one, grad_gain_one, grad_bias_one = norm_backward(upstream.astype(jnp.float32), gain_one, scaled_one, spread_one, normed_one)
    back_one = back_one.astype(jnp.bfloat16)
    grad_conv_one = jnp.concatenate([jnp.dot(first_tap.T, back_one, preferred_element_type=jnp.float32), jnp.dot(second_tap.T, back_one, preferred_element_type=jnp.float32), jnp.dot(third_tap.T, back_one, preferred_element_type=jnp.float32)], axis=0)
    to_first = jnp.dot(back_one, conv_one[:width].T, preferred_element_type=jnp.float32)
    to_second = jnp.dot(back_one, conv_one[width:2 * width].T, preferred_element_type=jnp.float32)
    to_third = jnp.dot(back_one, conv_one[2 * width:].T, preferred_element_type=jnp.float32)
    even_grad = to_first + jnp.concatenate([jnp.zeros((1, width), jnp.float32), to_third[:-1]], axis=0)
    frame_grad = jnp.stack([even_grad, to_second], axis=1).reshape(2 * frames_one, width)
    return (act_one.astype(jnp.bfloat16), grad_conv_one, grad_gain_one, grad_bias_one, frame_grad, to_third[-1:])

def assemble(audio_blocks, send_list, place_list):
    source = place_list // CAP
    slot_ids = place_list % CAP
    store_ids = jnp.arange(N_SEQ, dtype=jnp.int32)[:, None, None]
    dest_ids = jnp.arange(N_DP, dtype=jnp.int32)[None, :, None]
    local_ids = send_list[store_ids, source, dest_ids * CAP + slot_ids]
    gathered = audio_blocks[source, store_ids * ROWS + local_ids]
    return jnp.transpose(gathered, (1, 0, 2, 3)).reshape(N_DP, N_SEQ * ROWS * BLEN)

def reference(audio_blocks, send_list, place_list, cotangent, conv_zero, conv_one, gain_zero, bias_zero, gain_one, bias_one):
    waveforms = assemble(audio_blocks, send_list, place_list)

    def utterance(totals, inputs):
        waveform, upstream = inputs
        frames_zero = waveform.shape[0] // 5
        padded = jnp.concatenate([waveform, jnp.zeros((5,), jnp.bfloat16)])
        patches = frame_patches(padded, frames_zero)
        pre_zero = jnp.dot(patches, conv_zero, preferred_element_type=jnp.float32)
        act_zero, scaled_zero, spread_zero, normed_zero = norm_forward(pre_zero, gain_zero, bias_zero)
        frames_in = jnp.concatenate([act_zero.astype(jnp.bfloat16), jnp.zeros((1, C), jnp.bfloat16)], axis=0)
        feats, grad_one, gain_one_grad, bias_one_grad, frame_grad, tail_grad = layer_one(frames_in, frames_zero // 2, conv_one, gain_one, bias_one, upstream)
        back_zero, gain_zero_grad, bias_zero_grad = norm_backward(frame_grad, gain_zero, scaled_zero, spread_zero, normed_zero)
        grad_zero = jnp.dot(patches.astype(jnp.float32).T, back_zero, precision=lax.Precision.HIGHEST)
        totals = (totals[0] + grad_one, totals[1] + grad_zero, totals[2] + gain_zero_grad, totals[3] + bias_zero_grad, totals[4] + gain_one_grad, totals[5] + bias_one_grad)
        return (totals, feats)
    start = (jnp.zeros((3 * C, C), jnp.float32), jnp.zeros((10, C), jnp.float32), jnp.zeros((C,), jnp.float32), jnp.zeros((C,), jnp.float32), jnp.zeros((C,), jnp.float32), jnp.zeros((C,), jnp.float32))
    totals, features = lax.scan(utterance, start, (waveforms, cotangent))
    return (features, totals[0], totals[1], totals[2], totals[3], totals[4], totals[5])
```

```python
import functools

import jax
import jax.numpy as jnp
from jax import lax
from jax.experimental import pallas as pl
from jax.experimental.pallas import tpu as pltpu
from jax.sharding import PartitionSpec as P

norm_eps = 1e-05
f32 = jnp.float32
bf16 = jnp.bfloat16
tile_rows = 32
lanes = 128
hop = 10


def dot(a, b):
    return jnp.dot(a, b, preferred_element_type=f32)


def dot_rows(a, b):
    return lax.dot_general(a, b, (((0,), (0,)), ((), ())), preferred_element_type=f32)


def dot_lanes(a, b):
    return lax.dot_general(a, b, (((1,), (1,)), ((), ())), preferred_element_type=f32)


def iota(shape, dim):
    return lax.broadcasted_iota(jnp.int32, shape, dim)


def rounded(value):
    return value.astype(bf16)


def row_mean(value):
    return jnp.mean(value, axis=-1, keepdims=True)


def norm_parts(pre_act, gain, bias):
    center = pre_act - row_mean(pre_act)
    spread = lax.rsqrt(row_mean(center * center) + norm_eps)
    scaled = center * spread
    return scaled, spread, scaled * gain + bias


def gelu_parts(normed):
    cdf = 0.5 + 0.5 * lax.erf(normed * 0.7071067811865476)
    density = jnp.exp(-0.5 * normed * normed) * 0.3989422804014327
    return normed * cdf, cdf + normed * density


def norm_back(inner, gain, scaled, spread):
    pushed = inner * gain
    return spread * (pushed - row_mean(pushed) - scaled * row_mean(pushed * scaled))


def fold_rows(value):
    return jnp.sum(value.reshape(-1, 8, value.shape[-1]), axis=0)


def whole(*shape):
    return pl.BlockSpec(shape, lambda *_: (0,) * len(shape))


def call(body, outs, *args, limit=48 << 20, scratch=(), cost=None):
    return pl.pallas_call(
        body,
        out_shape=[jax.ShapeDtypeStruct(s, t) for s, t in outs],
        in_specs=[pl.BlockSpec(memory_space=pltpu.VMEM)] * len(args),
        out_specs=[pl.BlockSpec(memory_space=pltpu.VMEM)] * len(outs),
        scratch_shapes=list(scratch),
        compiler_params=pltpu.CompilerParams(vmem_limit_bytes=limit),
        cost_estimate=cost,
    )(*args)


def pack_body(blocks_ref, sends_ref, place_ref, own_ref, head_ref):
    rows, length = blocks_ref.shape
    width = own_ref.shape[1]
    slots = sends_ref.shape[1]
    mark = length % lanes
    hit = sends_ref[...] == iota((rows, slots), 0)
    spot = jnp.sum(jnp.where(hit, iota((rows, slots), 1).astype(f32), 0.0), axis=1, keepdims=True)
    blocks = blocks_ref[...].astype(f32)
    if width > length:
        blocks = jnp.concatenate([blocks, jnp.zeros((rows, width - length), f32)], axis=1)
    lane = iota((rows, width), 1)
    own_ref[...] = rounded(jnp.where(lane == length + hop, spot, blocks))
    lane = iota((rows, lanes), 1)
    moved = pltpu.roll(blocks[:, :lanes], mark, 1)
    first = place_ref[0:1, 0:1].astype(f32)
    head = jnp.where((lane >= mark) & (lane < mark + hop), moved, 0.0)
    head = jnp.where(lane == mark + hop + 1, spot, head)
    head_ref[...] = rounded(jnp.where(lane == mark + hop + 2, first, head))


def join_body(own_ref, pair_ref, head_ref, pair_head_ref, out_ref):
    base = own_ref.shape[1] - lanes
    for k, (main, head) in enumerate(((own_ref, head_ref), (pair_ref, pair_head_ref))):
        if base:
            out_ref[k, :, :base] = main[:, :base]
        out_ref[k, :, base:] = main[:, base:] + head[...]


def swap(value, axis, mask):
    count = lax.axis_size(axis)
    return lax.ppermute(value, axis, [(i, i ^ mask) for i in range(count)])


def gather_blocks(blocks, sends, place):
    n_data, n_time = lax.axis_size("dp"), lax.axis_size("seq")
    rows, length = blocks.shape
    width = -(-(length + hop + 3) // lanes) * lanes
    own, head = call(pack_body, [((rows, width), bf16), ((rows, lanes), bf16)], blocks, sends, place)
    pair = swap(own, "dp", 1)

    def from_next(mask):
        route = [
            (i * n_time + s + 1, (i ^ mask) * n_time + s)
            for i in range(n_data)
            for s in range(n_time - 1)
        ]
        return lax.ppermute(head, ("dp", "seq"), route)

    (table,) = call(
        join_body, [((2, rows, width), bf16)], own, pair, from_next(0), from_next(1)
    )
    mask = 2
    while mask < n_data:
        table = jnp.concatenate([table, swap(table, "dp", mask)], axis=0)
        mask *= 2
    return table.reshape(n_data * rows, width)


def assemble(table_ref, place_ref, after_ref, here, rows, length, capacity, frames):
    total, width = table_ref.shape
    chunk = min(total, 128)
    per_block = length // hop
    mark = length + hop
    shift = (iota((lanes, width), 1) == iota((lanes, width), 0) + length) & (
        iota((lanes, width), 0) < hop
    )
    shift = rounded(jnp.where(shift, 1.0, 0.0))
    lane = iota((chunk, width), 1)
    wanted = table_ref[0:1, mark + 2 : mark + 3].astype(f32).astype(jnp.int32)
    low = here * capacity

    def coded(start, column):
        spot = table_ref[pl.ds(start, chunk), column : column + 1].astype(f32).astype(jnp.int32)
        source = lax.div(iota((chunk, 1), 0) + start, rows) ^ here
        return jnp.where((spot >= low) & (spot < low + capacity), source * capacity + spot - low, -1)

    def one(step, carry):
        samples, after = carry
        start = pl.multiple_of(step * chunk, chunk) if total > chunk else 0
        part = table_ref[pl.ds(start, chunk), :]
        code = coded(start, mark)
        pick = rounded(jnp.where(code == place_ref[...], 1.0, 0.0))
        pick_after = rounded(jnp.where(code == after_ref[...], 1.0, 0.0))
        blocks = jnp.where(lane < length, part, jnp.zeros_like(part))
        heads = rounded(dot(part[:, :lanes], shift))
        samples = samples + dot_rows(pick, blocks) + dot_rows(pick_after, heads)
        match = (coded(start, mark + 1) == wanted) & (lane >= length) & (lane < mark)
        after = after + jnp.sum(jnp.where(match, part.astype(f32), 0.0), axis=0, keepdims=True)
        return samples, after

    carry = (jnp.zeros((frames, width), f32), jnp.zeros((1, width), f32))
    if total == chunk:
        samples, after = one(0, carry)
    else:
        samples, after = lax.fori_loop(0, total // chunk, one, carry)
    row = iota((frames, 1), 0)
    samples = samples + jnp.where(row >= frames - per_block, after, 0.0)
    window = iota((frames, width), 1) - hop * lax.rem(row, per_block)
    even = rounded(jnp.where((window >= 0) & (window < hop), samples, 0.0))
    odd = rounded(jnp.where((window >= hop // 2) & (window < hop + hop // 2), samples, 0.0))
    extra = rounded(jnp.where(iota((16, 1), 0) == 0, after, 0.0))
    return even, odd, extra


def layers_body(
    rows,
    length,
    capacity,
    split,
    table_ref,
    place_ref,
    after_ref,
    cotangent_ref,
    conv_even_ref,
    conv_odd_ref,
    conv_one_ref,
    params_ref,
    feats_ref,
    small_ref,
    *rest,
):
    sent_ref, keep_ref = rest[:2] if split else (None, None)
    (
    grad_ref,
    patch_even,
    patch_odd,
    pre_even,
    pre_odd,
    scaled_even,
    scaled_odd,
    slope_even,
    slope_odd,
    spread_even,
    spread_odd,
    act_wide,
    act_even,
    act_odd,
    act_next,
    back_wide,
    back_one,
    back_prev,
    high_even,
    high_odd,
    low_even,
    low_odd,
    ) = rest[2:] if split else rest
    here = lax.axis_index("dp")
    keep = jnp.where(lax.axis_index("seq") < lax.axis_size("seq") - 1, 1.0, 0.0)
    frames, width = feats_ref.shape
    gain_zero, bias_zero = params_ref[0:1, :], params_ref[1:2, :]
    gain_one, bias_one = params_ref[2:3, :], params_ref[3:4, :]

    even, odd, extra = assemble(
        table_ref, place_ref, after_ref, here, rows, length, capacity, frames
    )
    patch_even[...] = even
    patch_odd[...] = odd
    pre_even[...] = dot(even, conv_even_ref[...])
    pre_odd[...] = dot(odd, conv_odd_ref[...])

    def forward_zero(step, carry):
        at = pl.ds(pl.multiple_of(step * tile_rows, tile_rows), tile_rows)
        for pre, scaled_ref, slope_ref, spread_ref, act in (
            (pre_even, scaled_even, slope_even, spread_even, act_even),
            (pre_odd, scaled_odd, slope_odd, spread_odd, act_odd),
        ):
            scaled, spread, normed = norm_parts(pre[at, :], gain_zero, bias_zero)
            value, slope = gelu_parts(normed)
            scaled_ref[at, :] = scaled
            slope_ref[at, :] = slope
            spread_ref[at, :] = jnp.broadcast_to(spread, (tile_rows, lanes))
            act[at, :] = rounded(value)
            if act is act_even:
                act_wide[at, :] = value
        return carry

    lax.fori_loop(0, frames // tile_rows, forward_zero, 0)

    pre_extra = dot(extra, conv_even_ref[...])[:8]
    scaled_extra, spread_extra, normed_extra = norm_parts(pre_extra, gain_zero, bias_zero)
    value_extra, slope_extra = gelu_parts(normed_extra)
    act_wide[pl.ds(frames, 8), :] = value_extra * keep
    act_next[...] = rounded(act_wide[pl.ds(1, frames), :])

    pre_even[...] = (
        dot(act_even[...], conv_one_ref[0:width, :])
        + dot(act_odd[...], conv_one_ref[width : 2 * width, :])
        + dot(act_next[...], conv_one_ref[2 * width :, :])
    )
    back_wide[0:8, :] = jnp.zeros((8, width), f32)
    back_wide[pl.ds(frames + 8, 8), :] = jnp.zeros((8, width), f32)

    def layer_one(step, carry):
        gain_sum, bias_sum = carry
        at = pl.ds(pl.multiple_of(step * tile_rows, tile_rows), tile_rows)
        scaled, spread, normed = norm_parts(pre_even[at, :], gain_one, bias_one)
        value, slope = gelu_parts(normed)
        feats_ref[at, :] = rounded(value)
        inner = cotangent_ref[at, :].astype(f32) * slope
        back = norm_back(inner, gain_one, scaled, spread)
        back_one[at, :] = rounded(back)
        back_wide[pl.ds(pl.multiple_of(step * tile_rows + 8, 8), tile_rows), :] = back
        return gain_sum + fold_rows(inner * scaled), bias_sum + fold_rows(inner)

    zero = jnp.zeros((8, width), f32)
    gain_sum, bias_sum = lax.fori_loop(0, frames // tile_rows, layer_one, (zero, zero))
    small_ref[...] = jnp.zeros(small_ref.shape, f32)
    small_ref[12:13, :] = jnp.sum(gain_sum, axis=0, keepdims=True)
    small_ref[13:14, :] = jnp.sum(bias_sum, axis=0, keepdims=True)

    back_prev[...] = rounded(back_wide[pl.ds(7, frames), :])
    back = back_one[...]
    grad_ref[0:width, :] = dot_rows(act_even[...], back).astype(grad_ref.dtype)
    grad_ref[width : 2 * width, :] = dot_rows(act_odd[...], back).astype(grad_ref.dtype)
    grad_ref[2 * width :, :] = dot_rows(act_next[...], back).astype(grad_ref.dtype)
    pre_even[...] = dot_lanes(back, conv_one_ref[0:width, :]) + dot_lanes(
        back_prev[...], conv_one_ref[2 * width :, :]
    )
    pre_odd[...] = dot_lanes(back, conv_one_ref[width : 2 * width, :])
    tail = jnp.concatenate([back_wide[pl.ds(frames + 7, 8), :], zero], axis=0)
    grad_extra = dot_lanes(rounded(tail), conv_one_ref[2 * width :, :])[:8] * keep

    def backward_zero(step, carry):
        gain_sum, bias_sum = carry
        at = pl.ds(pl.multiple_of(step * tile_rows, tile_rows), tile_rows)
        for upstream, scaled_ref, slope_ref, spread_ref, high_ref, low_ref in (
            (pre_even, scaled_even, slope_even, spread_even, high_even, low_even),
            (pre_odd, scaled_odd, slope_odd, spread_odd, high_odd, low_odd),
        ):
            scaled = scaled_ref[at, :]
            inner = upstream[at, :] * slope_ref[at, :]
            back = norm_back(inner, gain_zero, scaled, spread_ref[at, 0:1])
            high = rounded(back)
            high_ref[at, :] = high
            low_ref[at, :] = rounded(back - high.astype(f32))
            gain_sum = gain_sum + fold_rows(inner * scaled)
            bias_sum = bias_sum + fold_rows(inner)
        return gain_sum, bias_sum

    inner = grad_extra * slope_extra
    back_extra = norm_back(inner, gain_zero, scaled_extra, spread_extra)
    gain_sum, bias_sum = lax.fori_loop(
        0, frames // tile_rows, backward_zero, (inner * scaled_extra, inner)
    )
    small_ref[10:11, :] = jnp.sum(gain_sum, axis=0, keepdims=True)
    small_ref[11:12, :] = jnp.sum(bias_sum, axis=0, keepdims=True)

    wide = table_ref.shape[1]
    tap = iota((wide, lanes), 1)
    place = iota((wide, lanes), 0)
    pick_even = rounded(jnp.where((lax.rem(place, hop) == tap) & (tap < hop), 1.0, 0.0))
    pick_odd = rounded(
        jnp.where((lax.rem(place + hop // 2, hop) == tap) & (tap < hop), 1.0, 0.0)
    )
    taps_even = rounded(dot(patch_even[...], pick_even))
    taps_odd = rounded(dot(patch_odd[...], pick_odd))
    taps_extra = rounded(dot(extra, pick_even))
    back_extra = jnp.concatenate([back_extra, zero], axis=0)
    high_extra = rounded(back_extra)
    low_extra = rounded(back_extra - high_extra.astype(f32))
    grad_zero = (
        dot_rows(taps_even, high_even[...])
        + dot_rows(taps_even, low_even[...])
        + dot_rows(taps_odd, high_odd[...])
        + dot_rows(taps_odd, low_odd[...])
        + dot_rows(taps_extra, high_extra)
        + dot_rows(taps_extra, low_extra)
    )
    small_ref[0:hop, :] = grad_zero[0:hop, :]
    if split:
        core, _, _ = chip_bits()
        share = keep_ref.shape[0] // 4
        for k in range(4):
            rows_at = pl.ds(k * share, share)
            keep_ref[rows_at, :] = grad_ref[at_share(2 * k + core, share), :]
            sent_ref[rows_at, :] = grad_ref[at_share(2 * k + 1 - core, share), :]
        store_small(sent_ref, 4 * share, small_ref[...])


def run_layers(table, place, cotangent, conv_zero, conv_one, params, rows, length, capacity, split):
    frames, width = cotangent.shape
    per_block = length // hop
    place_here = jnp.repeat(place, per_block)[None]
    place_after = jnp.repeat(jnp.concatenate([place[1:], jnp.full((1,), -2, place.dtype)]), per_block)[None]
    span = table.shape[1]
    copies = -(-span // hop) + 1
    tiled = jnp.tile(conv_zero, (copies, 1))
    conv_even = tiled[:span]
    conv_odd = tiled[hop // 2 : hop // 2 + span]
    wide = pltpu.VMEM((frames, width), f32)
    half = pltpu.VMEM((frames, width), bf16)
    patch = pltpu.VMEM((frames, span), bf16)
    column = pltpu.VMEM((frames, lanes), f32)
    scratch = (
        [patch] * 2
        + [wide] * 6
        + [column] * 2
        + [pltpu.VMEM((frames + 8, width), f32)]
        + [half] * 3
        + [pltpu.VMEM((frames + 16, width), f32)]
        + [half] * 6
    )
    outs = [((frames, width), bf16), ((small_rows, width), f32)]
    if split:
        count = 3 * width // 2
        outs += [((count + 2 * small_rows, width), bf16), ((count, width), bf16)]
        scratch = [pltpu.VMEM((3 * width, width), bf16)] + scratch
    else:
        outs += [((3 * width, width), f32)]
    return call(
        functools.partial(layers_body, rows, length, capacity, split),
        outs,
        table,
        place_here,
        place_after,
        cotangent,
        conv_even,
        conv_odd,
        conv_one,
        params,
        scratch=scratch,
    )


small_rows = 16


def wide_split(small):
    high = rounded(small)
    return high, rounded(small - high.astype(f32))


def store_small(ref, start, small):
    parts = wide_split(small)
    width = ref.shape[1]
    for column in range(0, small.shape[1], width):
        for part in parts:
            ref[pl.ds(start, small_rows), :] = part[:, column : column + width]
            start += small_rows


def add_small(ref, start, small):
    width = ref.shape[1]
    columns = []
    for _ in range(0, small.shape[1], width):
        high, low = ref[pl.ds(start, small_rows), :], ref[pl.ds(start + small_rows, small_rows), :]
        columns.append(high.astype(f32) + low.astype(f32))
        start += 2 * small_rows
    high, low = wide_split(small)
    return (high.astype(f32) + low.astype(f32)) + jnp.concatenate(columns, axis=1)


def chip_bits():
    spot = lax.axis_index("dp")
    return spot & 1, (spot >> 1) & 1, (spot >> 2) & 1


def at_share(index, share):
    return pl.ds(pl.multiple_of(index * share, share), share)


def core_body(keep_ref, got_ref, small_ref, sl_ref, sr_ref, kl_ref, kr_ref, small_out):
    _, near, far = chip_bits()
    half = sl_ref.shape[1]
    share = keep_ref.shape[0] // 4
    left, right = slice(0, half), slice(half, 2 * half)

    def total(far, near, columns):
        at = at_share(2 * far + near, share)
        return keep_ref[at, columns].astype(f32) + got_ref[at, columns].astype(f32)

    for k in range(2):
        rows = pl.ds(k * share, share)
        sl_ref[rows, :] = rounded(total(k, 1 - near, left))
        sr_ref[rows, :] = rounded(total(1 - far, k, right))
        kl_ref[rows, :] = total(k, near, left)
        kr_ref[rows, :] = total(far, k, right)
    small = add_small(got_ref, 4 * share, small_ref[...])
    small_out[...] = small
    store_small(sl_ref, 2 * share, small)


def chip_body(kl_ref, kr_ref, gl_ref, gr_ref, small_ref, sl_ref, sr_ref, ol_ref, or_ref, small_out):
    _, near, far = chip_bits()
    share = ol_ref.shape[0]

    def total(keep_ref, got_ref, index):
        at = at_share(index, share)
        return keep_ref[at, :] + got_ref[at, :].astype(f32)

    sl_ref[0:share, :] = rounded(total(kl_ref, gl_ref, 1 - far))
    sr_ref[...] = rounded(total(kr_ref, gr_ref, 1 - near))
    ol_ref[...] = total(kl_ref, gl_ref, far)
    or_ref[...] = total(kr_ref, gr_ref, near)
    small = add_small(gl_ref, 2 * share, small_ref[...])
    small_out[...] = small
    store_small(sl_ref, share, small)


def time_body(kl_ref, kr_ref, gl_ref, gr_ref, small_ref, sl_ref, sr_ref, small_out):
    share = sr_ref.shape[0]
    rows = pl.ds(0, share)
    sl_ref[rows, :] = rounded(kl_ref[rows, :].astype(f32) + gl_ref[rows, :].astype(f32))
    sr_ref[...] = rounded(kr_ref[...].astype(f32) + gr_ref[...].astype(f32))
    small = add_small(gl_ref, share, small_ref[...])
    small_out[...] = small
    store_small(sl_ref, share, small)


def last_body(kl_ref, kr_ref, gl_ref, gr_ref, small_ref, grad_ref, small_out):
    share, half = kr_ref.shape
    rows = pl.ds(0, share)
    grad_ref[:, :half] = kl_ref[rows, :].astype(f32) + gl_ref[rows, :].astype(f32)
    grad_ref[:, half:] = kr_ref[...].astype(f32) + gr_ref[...].astype(f32)
    small_out[...] = add_small(gl_ref, share, small_ref[...])


def sum_over_block(sent, keep, small):
    share, half = keep.shape[0] // 4, keep.shape[1] // 2
    tail = 2 * small_rows * 2
    kept_small = (small.shape, f32)

    def kind(count, extra, dtype):
        return ((count * share + extra, half), dtype)

    got = swap(sent, "dp", 1)
    sl, sr, kl, kr, small = call(
        core_body,
        [kind(2, tail, bf16), kind(2, 0, bf16), kind(2, 0, f32), kind(2, 0, f32), kept_small],
        keep, got, small,
    )
    gl, gr = swap(sl, "dp", 2), swap(sr, "dp", 4)
    sl, sr, kl, kr, small = call(
        chip_body,
        [kind(1, tail, bf16), kind(1, 0, bf16), kind(1, 0, f32), kind(1, 0, f32), kept_small],
        kl, kr, gl, gr, small,
    )
    gl, gr = swap(sl, "dp", 4), swap(sr, "dp", 2)
    sums = [kind(1, tail, bf16), kind(1, 0, bf16), kept_small]
    sl, sr, small = call(time_body, sums, kl, kr, gl, gr, small)
    gl, gr = swap(sl, "seq", 1), swap(sr, "seq", 2)
    sl, sr, small = call(time_body, sums, sl, sr, gl, gr, small)
    gl, gr = swap(sl, "seq", 2), swap(sr, "seq", 1)
    return call(last_body, [((share, 2 * half), f32), kept_small], sl, sr, gl, gr, small)


def on_device(
    audio_blocks,
    send_list,
    place_list,
    cotangent,
    conv_zero,
    conv_one,
    gain_zero,
    bias_zero,
    gain_one,
    bias_one,
):
    n_data, n_time = lax.axis_size("dp"), lax.axis_size("seq")
    blocks = audio_blocks[0]
    rows, length = blocks.shape
    capacity = send_list.shape[2] // n_data
    small_block = n_data == 8 and n_time == 4
    table = gather_blocks(blocks, send_list[0], place_list[0])
    params = jnp.stack([gain_zero, bias_zero, gain_one, bias_one])
    feats, small, *grads = run_layers(
        table,
        place_list[0, 0],
        cotangent[0],
        conv_zero,
        conv_one,
        params,
        rows,
        length,
        capacity,
        small_block,
    )
    if small_block:
        grad, small = sum_over_block(*grads, small)
    else:
        grad = lax.psum_scatter(grads[0], "dp", scatter_dimension=0, tiled=True)
        grad = lax.psum(grad, "seq")
        small = lax.psum(small, ("dp", "seq"))
    return (feats[None], grad, small[0:hop], small[10], small[11], small[12], small[13])


def solution(mesh):
    placed = (
        P("dp", "seq", None),
        P("seq", "dp", None),
        P("seq", "dp", None),
        P("dp", "seq", None),
        P(),
        P(),
        P(),
        P(),
        P(),
        P(),
    )
    return jax.shard_map(
        on_device,
        mesh=mesh,
        in_specs=placed,
        out_specs=(P("dp", "seq", None), P("dp", None), P(), P(), P(), P(), P()),
        check_vma=False,
    )
```

```python
import functools

import jax
import jax.numpy as jnp
from jax import lax
from jax.experimental import pallas as pl
from jax.experimental.pallas import tpu as pltpu
from jax.sharding import PartitionSpec as P

norm_eps = 1e-05
f32 = jnp.float32
bf16 = jnp.bfloat16
tail_rows = 16
small_rows = 16
lanes = 128
hop = 10


def dot(a, b):
    return jnp.dot(a, b, preferred_element_type=f32)


def dot_rows(a, b):
    return lax.dot_general(a, b, (((0,), (0,)), ((), ())), preferred_element_type=f32)


def dot_lanes(a, b):
    return lax.dot_general(a, b, (((1,), (1,)), ((), ())), preferred_element_type=f32)


def iota(shape, dim):
    return lax.broadcasted_iota(jnp.int32, shape, dim)


def rounded(value):
    return value.astype(bf16)


def row_mean(value):
    return jnp.mean(value, axis=-1, keepdims=True)


def norm_parts(pre_act, gain, bias):
    center = pre_act - row_mean(pre_act)
    spread = lax.rsqrt(row_mean(center * center) + norm_eps)
    scaled = center * spread
    return scaled, spread, scaled * gain + bias


def gelu_parts(normed):
    cdf = 0.5 + 0.5 * lax.erf(normed * 0.7071067811865476)
    density = jnp.exp2(normed * normed * -0.7213475204444817) * 0.3989422804014327
    return normed * cdf, cdf + normed * density


def norm_back(inner, gain, scaled, spread):
    pushed = inner * gain
    return spread * (pushed - row_mean(pushed) - scaled * row_mean(pushed * scaled))


def call(body, outs, *args, scratch=(), spaces=None, flops=0):
    spaces = spaces or [pltpu.VMEM] * len(args)
    size = sum(a.size * a.dtype.itemsize for a in args)
    return pl.pallas_call(
        body,
        out_shape=[jax.ShapeDtypeStruct(s, t) for s, t in outs],
        in_specs=[pl.BlockSpec(memory_space=space) for space in spaces],
        out_specs=[pl.BlockSpec(memory_space=pltpu.VMEM)] * len(outs),
        scratch_shapes=list(scratch),
        compiler_params=pltpu.CompilerParams(vmem_limit_bytes=40 << 20),
        cost_estimate=pl.CostEstimate(flops=flops, bytes_accessed=size, transcendentals=0),
    )(*args)


def swap(value, mask):
    count = lax.axis_size("dp")
    return lax.ppermute(value, "dp", [(i, i ^ mask) for i in range(count)])


def swap_time(value, mask):
    count = lax.axis_size("seq")
    return lax.ppermute(value, "seq", [(i, i ^ mask) for i in range(count)])


def pack_body(blocks_ref, sends_ref, own_ref, blocks_here, sends_here, sems):
    copies = [
        pltpu.make_async_copy(blocks_ref, blocks_here, sems.at[0]),
        pltpu.make_async_copy(sends_ref, sends_here, sems.at[1]),
    ]
    for copy in copies:
        copy.start()
    for copy in copies:
        copy.wait()
    rows, length = blocks_here.shape
    width = own_ref.shape[1]
    slots = sends_here.shape[1]
    hit = sends_here[...] == iota((rows, slots), 0)
    spot = jnp.sum(jnp.where(hit, iota((rows, slots), 1).astype(f32), 0.0), axis=1, keepdims=True)
    blocks = blocks_here[...].astype(f32)
    blocks = jnp.concatenate([blocks, jnp.zeros((rows, width - length), f32)], axis=1)
    own_ref[...] = rounded(jnp.where(iota((rows, width), 1) == length, spot, blocks))


def join_body(a_ref, b_ref, out_ref):
    out_ref[...] = jnp.concatenate([a_ref[...], b_ref[...]], axis=0)


def gather_blocks(blocks, sends):
    rows, length = blocks.shape
    width = -(-(length + hop) // lanes) * lanes
    scratch = [
        pltpu.VMEM(blocks.shape, bf16),
        pltpu.VMEM(sends.shape, sends.dtype),
        pltpu.SemaphoreType.DMA((2,)),
    ]
    (table,) = call(
        pack_body, [((rows, width), bf16)], blocks, sends, scratch=scratch, spaces=[pl.ANY] * 2
    )
    mask, step = 1, 1
    while step < lax.axis_size("dp"):
        got = swap(table, mask)
        step *= 2
        mask = step | 1
        if step < lax.axis_size("dp"):
            (table,) = call(join_body, [((rows * step, width), bf16)], table, got)
    return table, got


def assemble_body(rows, length, capacity, place_ref, table_ref, got_ref, samples_ref, head_ref):
    here = lax.axis_index("dp")
    half, width = table_ref.shape
    frames = samples_ref.shape[0]
    chunk = min(half, 128)
    per_block = length // hop
    row = iota((lanes, width), 0)
    shift = rounded(jnp.where((iota((lanes, width), 1) == row + length) & (row < hop), 1.0, 0.0))
    lane = iota((chunk, width), 1)
    low = here * capacity
    block = lax.div(iota((1, frames), 1), per_block)
    place = jnp.full((1, frames), -2, jnp.int32)
    after = place
    for r in range(place_ref.shape[1]):
        place = jnp.where(block == r, place_ref[0, r], place)
        after = jnp.where(block == r - 1, place_ref[0, r], after)

    def slot_source(slot):
        parity = jnp.zeros_like(slot)
        bits = 2
        while bits < 2 * half // rows:
            parity = parity ^ jnp.where((slot & bits) != 0, 1, 0)
            bits *= 2
        return slot ^ parity ^ here

    def part_samples(ref, first, start):
        part = ref[pl.ds(start, chunk), :]
        spot = part[:, length : length + 1].astype(f32).astype(jnp.int32)
        source = slot_source(lax.div(iota((chunk, 1), 0) + (start + first), rows))
        code = jnp.where(
            (spot >= low) & (spot < low + capacity), source * capacity + spot - low, -1
        )
        pick = rounded(jnp.where(code == place, 1.0, 0.0))
        pick_after = rounded(jnp.where(code == after, 1.0, 0.0))
        blocks = jnp.where(lane < length, part, jnp.zeros_like(part))
        heads = rounded(dot(part[:, :lanes], shift))
        return dot_rows(pick, blocks) + dot_rows(pick_after, heads)

    samples = jnp.zeros((frames, width), f32)
    for ref, first in ((table_ref, 0), (got_ref, half)):
        if half == chunk:
            samples = samples + part_samples(ref, first, 0)
        else:
            samples = lax.fori_loop(
                0,
                half // chunk,
                lambda i, s: s + part_samples(ref, first, pl.multiple_of(i * chunk, chunk)),
                samples,
            )
    samples_ref[...] = rounded(samples)
    head_ref[...] = rounded(samples[:tail_rows, :lanes])


def conv_body(length, conv_ref, even_ref, odd_ref):
    width = even_ref.shape[0]
    taps = conv_ref.shape[0]
    conv = conv_ref[...]
    for ref, offset in ((even_ref, 0), (odd_ref, hop // 2)):
        place = iota((width, taps), 0) + offset
        ref[...] = rounded(
            dot(rounded(jnp.where(lax.rem(place, hop) == iota((width, taps), 1), 1.0, 0.0)), conv)
        )


def windows(samples, start, per_block, offset):
    inside = iota(samples.shape, 1) - hop * lax.rem(iota((samples.shape[0], 1), 0) + start, per_block)
    inside = inside - offset
    return jnp.where((inside >= 0) & (inside < hop), samples, jnp.zeros_like(samples))


def rows_at(step, count):
    return pl.ds(pl.multiple_of(step * count, count), count)


def zero_forward_body(
    per_block, samples_ref, ce_ref, co_ref, gain_ref, bias_ref,
    act_even, act_odd, scaled_even, scaled_odd, slope_even, slope_odd, spread_even, spread_odd,
):
    samples = samples_ref[...]
    for conv, offset, act, scaled_ref, slope_ref, spread_ref in (
        (ce_ref, 0, act_even, scaled_even, slope_even, spread_even),
        (co_ref, hop // 2, act_odd, scaled_odd, slope_odd, spread_odd),
    ):
        pre = dot(windows(samples, 0, per_block, offset), conv[...])
        scaled, spread, normed = norm_parts(pre, gain_ref[...], bias_ref[...])
        value, slope = gelu_parts(normed)
        act[...] = rounded(value)
        scaled_ref[...] = scaled
        slope_ref[...] = slope
        spread_ref[...] = jnp.broadcast_to(spread, spread_ref.shape)


def layers_body(
    length, split,
    samples_ref, after_ref, ce_ref, co_ref, gain_zero_ref, bias_zero_ref,
    act_even, act_odd, cotangent_ref, conv_one_ref, gain_one_ref, bias_one_ref,
    feats_ref, back_one, back_prev, back_tail, fix_patch, fix_scaled, fix_slope, fix_spread,
    small_ref, *rest,
):
    keep = jnp.where(lax.axis_index("seq") < lax.axis_size("seq") - 1, 1.0, 0.0)
    frames, width = feats_ref.shape
    span = samples_ref.shape[1]
    per_block = length // hop
    if split:
        sent_ref, keep_ref, grad_ref, wide, act_last, act_next = rest
    else:
        grad_ref, wide, act_last, act_next = rest

    last = frames - tail_rows
    row = iota((lanes, span), 0)
    shift = rounded(jnp.where((iota((lanes, span), 1) == row + length) & (row < hop), keep, 0.0))
    after = dot(after_ref[...], shift)[0:1, :]
    patch_last = samples_ref[pl.ds(last, tail_rows), :].astype(f32)
    patch_last = windows(rounded(patch_last + jnp.where(iota((tail_rows, 1), 0) >= tail_rows - 1, after, 0.0)), last, per_block, hop // 2)
    patch_extra = rounded(jnp.where(iota((tail_rows, 1), 0) == 0, after, 0.0))
    fix_patch[0:tail_rows, :] = patch_last
    fix_patch[tail_rows:, :] = patch_extra
    pre = jnp.concatenate([dot(patch_last, co_ref[...]), dot(patch_extra, ce_ref[...])], axis=0)
    scaled, spread, normed = norm_parts(pre, gain_zero_ref[...], bias_zero_ref[...])
    value, slope = gelu_parts(normed)
    fix_scaled[...] = scaled
    fix_slope[...] = slope
    fix_spread[...] = jnp.broadcast_to(spread, fix_spread.shape)
    act_last[0:last, :] = act_odd[0:last, :]
    act_last[last:, :] = rounded(value[:tail_rows])
    wide[0:frames, :] = act_even[...].astype(f32)
    wide[pl.ds(frames, 8), :] = value[tail_rows : tail_rows + 8] * keep
    act_next[...] = rounded(wide[pl.ds(1, frames), :])

    pre = (
        dot(act_even[...], conv_one_ref[0:width, :])
        + dot(act_last[...], conv_one_ref[width : 2 * width, :])
        + dot(act_next[...], conv_one_ref[2 * width :, :])
    )
    scaled, spread, normed = norm_parts(pre, gain_one_ref[...], bias_one_ref[...])
    value, slope = gelu_parts(normed)
    feats_ref[...] = rounded(value)
    inner = cotangent_ref[...].astype(f32) * slope
    back = norm_back(inner, gain_one_ref[...], scaled, spread)
    back_one[...] = rounded(back)
    wide[0:8, :] = jnp.zeros((8, width), f32)
    wide[pl.ds(8, frames), :] = back
    small_ref[0:1, :] = jnp.sum(inner * scaled, axis=0, keepdims=True)
    small_ref[1:2, :] = jnp.sum(inner, axis=0, keepdims=True)

    back_prev[...] = rounded(wide[pl.ds(7, frames), :])
    first = iota((tail_rows, 1), 0) == 0
    back_tail[...] = rounded(jnp.where(first, wide[pl.ds(frames + 7, 1), :] * keep, 0.0))
    back = back_one[...]
    grad_ref[0:width, :] = dot_rows(act_even[...], back).astype(grad_ref.dtype)
    grad_ref[width : 2 * width, :] = dot_rows(act_last[...], back).astype(grad_ref.dtype)
    grad_ref[2 * width :, :] = dot_rows(act_next[...], back).astype(grad_ref.dtype)
    if split:
        core, _, _ = chip_bits()
        share = keep_ref.shape[0] // 4
        for k in range(4):
            at = pl.ds(k * share, share)
            keep_ref[at, :] = grad_ref[rows_at(2 * k + core, share), :]
            sent_ref[at, :] = grad_ref[rows_at(2 * k + 1 - core, share), :]


def zero_backward_body(
    length,
    samples_ref, fix_patch, conv_one_ref, gain_ref, back_one, back_prev, back_tail,
    scaled_even, scaled_odd, slope_even, slope_odd, spread_even, spread_odd,
    fix_scaled, fix_slope, fix_spread, small_one,
    small_ref,
):
    frames, width = back_one.shape
    span = samples_ref.shape[1]
    per_block = length // hop
    gain = gain_ref[...]
    last = frames - tail_rows
    back = back_one[...]
    third = conv_one_ref[2 * width :, :]
    up_even = dot_lanes(back, conv_one_ref[0:width, :]) + dot_lanes(back_prev[...], third)
    up_odd = dot_lanes(back, conv_one_ref[width : 2 * width, :])
    up_fix = jnp.concatenate([up_odd[last:], dot_lanes(back_tail[...], third)], axis=0)
    gain_sum, bias_sum, parts = 0.0, 0.0, []
    for up, scaled, slope, spread in (
        (up_even, scaled_even[...], slope_even[...], spread_even[:, 0:1]),
        (up_odd[:last], scaled_odd[0:last, :], slope_odd[0:last, :], spread_odd[0:last, 0:1]),
        (up_fix, fix_scaled[...], fix_slope[...], fix_spread[:, 0:1]),
    ):
        inner = up * slope
        back = norm_back(inner, gain, scaled, spread)
        high = rounded(back)
        parts.append((high, rounded(back - high.astype(f32))))
        gain_sum = gain_sum + jnp.sum(inner * scaled, axis=0, keepdims=True)
        bias_sum = bias_sum + jnp.sum(inner, axis=0, keepdims=True)

    tap = iota((span, lanes), 1)
    place = iota((span, lanes), 0)
    pick_even = rounded(jnp.where(lax.rem(place, hop) == tap, 1.0, 0.0))
    pick_odd = rounded(jnp.where(lax.rem(place + hop // 2, hop) == tap, 1.0, 0.0))
    samples = samples_ref[...]
    taps_even = rounded(dot(windows(samples, 0, per_block, 0), pick_even))
    taps_odd = rounded(dot(windows(samples, 0, per_block, hop // 2), pick_odd))
    taps_last = rounded(dot(fix_patch[0:tail_rows, :], pick_odd))
    taps_extra = rounded(dot(fix_patch[tail_rows:, :], pick_even))
    taps_fix = jnp.concatenate([taps_last, taps_extra], axis=0)
    grad = 0.0
    for taps, pair in zip((taps_even, taps_odd[:last], taps_fix), parts):
        for part in pair:
            grad = grad + dot_rows(taps, part)
    small_ref[...] = jnp.zeros(small_ref.shape, f32)
    small_ref[0:hop, :] = grad[0:hop, :]
    small_ref[hop : hop + 1, :] = gain_sum
    small_ref[hop + 1 : hop + 2, :] = bias_sum
    small_ref[hop + 2 : hop + 4, :] = small_one[0:2, :]


def run_layers(table, got, place, cotangent, conv_zero, conv_one, gains, rows, length, capacity, split):
    gain_zero, bias_zero, gain_one, bias_one = (g[None] for g in gains)
    frames, width = cotangent.shape
    span = table.shape[1]
    per_block = length // hop
    whole, half = ((frames, width), f32), ((frames, width), bf16)
    tail = 2 * tail_rows
    samples, head = call(
        functools.partial(assemble_body, rows, length, capacity),
        [((frames, span), bf16), ((tail_rows, lanes), bf16)],
        place, table, got,
        spaces=[pltpu.SMEM, pltpu.VMEM, pltpu.VMEM],
    )
    conv_even, conv_odd = call(
        functools.partial(conv_body, length), [((span, width), bf16)] * 2, conv_zero
    )
    count = lax.axis_size("seq")
    after = lax.ppermute(head, "seq", [(i + 1, i) for i in range(count - 1)])
    act_even, act_odd, *saved = call(
        functools.partial(zero_forward_body, per_block),
        [half] * 2 + [whole] * 4 + [((frames, lanes), f32)] * 2,
        samples, conv_even, conv_odd, gain_zero, bias_zero,
        flops=4 * 10**9,
    )
    outs = [half] * 3 + [
        ((tail_rows, width), bf16),
        ((tail, span), bf16),
        ((tail, width), f32),
        ((tail, width), f32),
        ((tail, lanes), f32),
        ((8, width), f32),
    ]
    grad = (3 * width, width)
    scratch = [
        pltpu.VMEM((frames + 16, width), f32),
        pltpu.VMEM(*half),
        pltpu.VMEM(*half),
    ]
    if split:
        outs += [((3 * width // 2, width), bf16)] * 2
        scratch = [pltpu.VMEM(grad, bf16)] + scratch
    else:
        outs += [(grad, f32)]
    feats, back_one, back_prev, back_tail, fix_patch, *others = call(
        functools.partial(layers_body, length, split),
        outs,
        samples, after, conv_even, conv_odd, gain_zero, bias_zero,
        act_even, act_odd, cotangent, conv_one, gain_one, bias_one,
        scratch=scratch,
        flops=6 * 10**9,
    )
    *fix, small_one = others[:4]
    (small,) = call(
        functools.partial(zero_backward_body, length),
        [((small_rows, width), f32)],
        samples, fix_patch, conv_one, gain_zero, back_one, back_prev, back_tail,
        *saved, *fix, small_one,
        flops=4 * 10**9,
    )
    return feats, small, *others[4:]


def wide_split(small):
    high = rounded(small)
    return high, rounded(small - high.astype(f32))


def store_small(ref, start, small):
    width = ref.shape[1]
    for column in range(0, small.shape[1], width):
        for part in wide_split(small):
            ref[pl.ds(start, small_rows), :] = part[:, column : column + width]
            start += small_rows


def add_small(ref, start, small):
    width = ref.shape[1]
    columns = []
    for _ in range(0, small.shape[1], width):
        high, low = ref[pl.ds(start, small_rows), :], ref[pl.ds(start + small_rows, small_rows), :]
        columns.append(high.astype(f32) + low.astype(f32))
        start += 2 * small_rows
    high, low = wide_split(small)
    return (high.astype(f32) + low.astype(f32)) + jnp.concatenate(columns, axis=1)


def chip_bits():
    spot = lax.axis_index("dp")
    return spot & 1, (spot >> 1) & 1, (spot >> 2) & 1


def core_body(left, keep_ref, got_ref, *refs):
    _, near, far = chip_bits()
    if left:
        small_ref, other_ref, sent_ref, kept_ref, small_out = refs
    else:
        sent_ref, kept_ref = refs
    half = kept_ref.shape[1]
    share = keep_ref.shape[0] // 4
    columns = slice(0, half) if left else slice(half, 2 * half)

    def total(k, mine):
        index = 2 * k + mine if left else 2 * mine + k
        at = rows_at(index, share)
        return keep_ref[at, columns].astype(f32) + got_ref[at, columns].astype(f32)

    mine = near if left else far
    for k in range(2):
        at = pl.ds(k * share, share)
        sent_ref[at, :] = rounded(total(k, 1 - mine))
        kept_ref[at, :] = total(k, mine)
    if left:
        small = small_ref[...] + other_ref[...]
        small_out[...] = small
        store_small(sent_ref, 2 * share, small)


def chip_body(left, kept_ref, got_ref, *refs):
    _, near, far = chip_bits()
    if left:
        small_ref, sent_ref, out_ref, small_out = refs
    else:
        sent_ref, out_ref = refs
    share = out_ref.shape[0]
    mine = far if left else near

    def total(index):
        at = rows_at(index, share)
        return kept_ref[at, :] + got_ref[at, :].astype(f32)

    sent_ref[0:share, :] = rounded(total(1 - mine))
    out_ref[...] = total(mine)
    if left:
        small = add_small(got_ref, 2 * share, small_ref[...])
        small_out[...] = small
        store_small(sent_ref, share, small)


def time_body(left, kept_ref, got_ref, *refs):
    if left:
        small_ref, sent_ref, small_out = refs
    else:
        (sent_ref,) = refs
    share = sent_ref.shape[0] - (4 * small_rows if left else 0)
    at = pl.ds(0, share)
    sent_ref[at, :] = rounded(kept_ref[at, :].astype(f32) + got_ref[at, :].astype(f32))
    if left:
        small = add_small(got_ref, share, small_ref[...])
        small_out[...] = small
        store_small(sent_ref, share, small)


def last_body(kl_ref, kr_ref, gl_ref, gr_ref, small_ref, grad_ref, small_out):
    share, half = kr_ref.shape
    at = pl.ds(0, share)
    grad_ref[:, :half] = kl_ref[at, :].astype(f32) + gl_ref[at, :].astype(f32)
    grad_ref[:, half:] = kr_ref[...].astype(f32) + gr_ref[...].astype(f32)
    small_out[...] = add_small(gl_ref, share, small_ref[...])


def sum_over_block(sent, keep, small):
    share, half = keep.shape[0] // 4, keep.shape[1] // 2
    tail = 4 * small_rows
    kept_small = (small.shape, f32)

    def kind(count, extra, dtype):
        return ((count * share + extra, half), dtype)

    def stage(body, count, left, *args):
        outs = [kind(count, tail if left else 0, bf16)]
        if body is not time_body:
            outs.append(kind(count, 0, f32))
        if left:
            outs.append(kept_small)
        return call(functools.partial(body, left), outs, *args)

    got = swap(sent, 1)
    other = swap(small, 1)
    sl, kl, small = stage(core_body, 2, True, keep, got, small, other)
    gl = swap(sl, 2)
    sr, kr = stage(core_body, 2, False, keep, got)
    gr = swap(sr, 4)
    sl, kl, small = stage(chip_body, 1, True, kl, gl, small)
    gl = swap(sl, 4)
    sr, kr = stage(chip_body, 1, False, kr, gr)
    gr = swap(sr, 2)
    sl, small = stage(time_body, 1, True, kl, gl, small)
    gl = swap_time(sl, 1)
    (sr,) = stage(time_body, 1, False, kr, gr)
    gr = swap_time(sr, 2)
    sl, small = stage(time_body, 1, True, sl, gl, small)
    gl = swap_time(sl, 2)
    (sr,) = stage(time_body, 1, False, sr, gr)
    gr = swap_time(sr, 1)
    return call(last_body, [((share, 2 * half), f32), kept_small], sl, sr, gl, gr, small)


def on_device(
    audio_blocks,
    send_list,
    place_list,
    cotangent,
    conv_zero,
    conv_one,
    gain_zero,
    bias_zero,
    gain_one,
    bias_one,
):
    n_data, n_time = lax.axis_size("dp"), lax.axis_size("seq")
    blocks = audio_blocks[0]
    rows, length = blocks.shape
    capacity = send_list.shape[2] // n_data
    small_block = n_data == 8 and n_time == 4
    table, got = gather_blocks(blocks, send_list[0])
    feats, small, *grads = run_layers(
        table,
        got,
        place_list[0],
        cotangent[0],
        conv_zero,
        conv_one,
        (gain_zero, bias_zero, gain_one, bias_one),
        rows,
        length,
        capacity,
        small_block,
    )
    if small_block:
        grad, small = sum_over_block(*grads, small)
    else:
        grad = lax.psum_scatter(grads[0], "dp", scatter_dimension=0, tiled=True)
        grad = lax.psum(grad, "seq")
        small = lax.psum(small, ("dp", "seq"))
    return (feats[None], grad, small[0:hop], *(small[hop + k] for k in range(4)))


def solution(mesh):
    placed = (
        P("dp", "seq", None),
        P("seq", "dp", None),
        P("seq", "dp", None),
        P("dp", "seq", None),
        P(),
        P(),
        P(),
        P(),
        P(),
        P(),
    )
    return jax.shard_map(
        on_device,
        mesh=mesh,
        in_specs=placed,
        out_specs=(P("dp", "seq", None), P("dp", None), P(), P(), P(), P(), P()),
        check_vma=False,
    )
```

```python
import functools

import jax
import jax.numpy as jnp
from jax import lax
from jax.experimental import pallas as pl
from jax.experimental.pallas import tpu as pltpu
from jax.sharding import PartitionSpec as P

norm_eps = 1e-05
f32 = jnp.float32
bf16 = jnp.bfloat16
tail_rows = 16
small_rows = 16
lanes = 128
hop = 10


def dot(a, b):
    return jnp.dot(a, b, preferred_element_type=f32)


def dot_rows(a, b):
    return lax.dot_general(a, b, (((0,), (0,)), ((), ())), preferred_element_type=f32)


def dot_lanes(a, b):
    return lax.dot_general(a, b, (((1,), (1,)), ((), ())), preferred_element_type=f32)


def iota(shape, dim):
    return lax.broadcasted_iota(jnp.int32, shape, dim)


def rounded(value):
    return value.astype(bf16)


def row_mean(value):
    return jnp.mean(value, axis=-1, keepdims=True)


def norm_parts(pre_act, gain, bias):
    center = pre_act - row_mean(pre_act)
    spread = lax.rsqrt(row_mean(center * center) + norm_eps)
    scaled = center * spread
    return scaled, spread, scaled * gain + bias


def gelu_parts(normed):
    cdf = 0.5 + 0.5 * lax.erf(normed * 0.7071067811865476)
    density = jnp.exp2(normed * normed * -0.7213475204444817) * 0.3989422804014327
    return normed * cdf, cdf + normed * density


def norm_back(inner, gain, scaled, spread):
    pushed = inner * gain
    return spread * (pushed - row_mean(pushed) - scaled * row_mean(pushed * scaled))


def call(body, outs, *args, scratch=(), spaces=None, flops=0, behind=None):
    spaces = spaces or [pltpu.VMEM] * len(args)
    args = [
        pltpu.with_memory_space_constraint(a, pltpu.HBM) if space == pltpu.HBM else a
        for a, space in zip(args, spaces)
    ]
    size = sum(a.size * a.dtype.itemsize for a in args)
    count = len(args)
    run = body
    if behind is not None:
        args, spaces = [*args, behind], [*spaces, pl.ANY]

        def run(*refs):
            body(*refs[:count], *refs[count + 1 :])

    return pl.pallas_call(
        run,
        out_shape=[jax.ShapeDtypeStruct(s, t) for s, t in outs],
        in_specs=[pl.BlockSpec(memory_space=space) for space in spaces],
        out_specs=[pl.BlockSpec(memory_space=pltpu.VMEM)] * len(outs),
        scratch_shapes=list(scratch),
        compiler_params=pltpu.CompilerParams(vmem_limit_bytes=40 << 20),
        cost_estimate=pl.CostEstimate(flops=flops, bytes_accessed=size, transcendentals=0),
    )(*args)


def swap(value, mask):
    count = lax.axis_size("dp")
    return lax.ppermute(value, "dp", [(i, i ^ mask) for i in range(count)])


def swap_time(value, mask):
    count = lax.axis_size("seq")
    return lax.ppermute(value, "seq", [(i, i ^ mask) for i in range(count)])


def pack_body(blocks_ref, sends_ref, own_ref, blocks_here, sends_here, sems):
    fetch((blocks_ref, sends_ref), (blocks_here, sends_here), sems)
    rows, length = blocks_here.shape
    width = own_ref.shape[1]
    slots = sends_here.shape[1]
    hit = sends_here[...] == iota((rows, slots), 0)
    spot = jnp.sum(jnp.where(hit, iota((rows, slots), 1).astype(f32), 0.0), axis=1, keepdims=True)
    blocks = blocks_here[...].astype(f32)
    blocks = jnp.concatenate([blocks, jnp.zeros((rows, width - length), f32)], axis=1)
    own_ref[...] = rounded(jnp.where(iota((rows, width), 1) == length, spot, blocks))


def join_body(a_ref, b_ref, out_ref):
    out_ref[...] = jnp.concatenate([a_ref[...], b_ref[...]], axis=0)


def gather_blocks(blocks, sends):
    rows, length = blocks.shape
    width = -(-(length + hop) // lanes) * lanes
    scratch = [
        pltpu.VMEM(blocks.shape, bf16),
        pltpu.VMEM(sends.shape, sends.dtype),
        pltpu.SemaphoreType.DMA((2,)),
    ]
    (table,) = call(
        pack_body, [((rows, width), bf16)], blocks, sends, scratch=scratch, spaces=[pltpu.HBM] * 2
    )
    mask, step = 1, 1
    while step < lax.axis_size("dp"):
        got = swap(table, mask)
        step *= 2
        mask = step | 1
        if step < lax.axis_size("dp"):
            (table,) = call(join_body, [((rows * step, width), bf16)], table, got)
    return table, got


def fetch(refs, buffers, sems):
    copies = [pltpu.make_async_copy(r, b, sems.at[k]) for k, (r, b) in enumerate(zip(refs, buffers))]
    for copy in copies:
        copy.start()
    for copy in copies:
        copy.wait()


def prepare_body(
    per_block,
    conv_hbm, place_hbm, *refs,
):
    vectors, (even_ref, odd_ref, place_ref, after_ref, gains_ref) = refs[:4], refs[4:9]
    conv_here, place_here, *vectors_here, sems = refs[9:]
    fetch((conv_hbm, place_hbm, *vectors), (conv_here, place_here, *vectors_here), sems)
    width = even_ref.shape[0]
    taps = conv_here.shape[0]
    conv = conv_here[...]
    for ref, offset in ((even_ref, 0), (odd_ref, hop // 2)):
        spot = iota((width, taps), 0) + offset
        ref[...] = rounded(
            dot(rounded(jnp.where(lax.rem(spot, hop) == iota((width, taps), 1), 1.0, 0.0)), conv)
        )
    frames = place_ref.shape[0]
    rows = place_here.shape[1]
    place = rounded(jnp.broadcast_to(place_here[...].astype(f32), (lanes, rows)))
    block = lax.div(iota((frames, rows), 0), per_block)
    for ref, offset in ((place_ref, 0), (after_ref, 1)):
        wanted = dot_lanes(rounded(jnp.where(block + offset == iota((frames, rows), 1), 1.0, 0.0)), place)
        ref[...] = jnp.where(iota((frames, 1), 0) + offset * per_block < frames, wanted, -2.0)
    gains_ref[...] = jnp.concatenate([v[...] for v in vectors_here] * 2, axis=0)


def assemble_body(rows, length, capacity, table_ref, got_ref, place_ref, after_ref, samples_ref, head_ref):
    here = lax.axis_index("dp")
    half, width = table_ref.shape
    frames = samples_ref.shape[0]
    chunk = 2 * half if 2 * half <= lanes else lanes
    row = iota((lanes, width), 0)
    shift = rounded(jnp.where((iota((lanes, width), 1) == row + length) & (row < hop), 1.0, 0.0))
    mark = rounded(jnp.where(iota((tail_rows, width), 1) == length, 1.0, 0.0))
    lane = iota((chunk, width), 1)
    low = here * capacity

    def part_samples(part, first):
        spot = dot_lanes(mark, part)[0:1, :].astype(jnp.int32)
        slot = lax.div(iota((1, chunk), 1) + first, rows)
        source, bits = slot ^ here, 2
        while bits < 2 * half // rows:
            source = source ^ jnp.where((slot & bits) != 0, 1, 0)
            bits *= 2
        mine = (spot >= low) & (spot < low + capacity)
        code = jnp.where(mine, source * capacity + spot - low, -1).astype(f32)
        pick = rounded(jnp.where(code == place_ref[:, :chunk], 1.0, 0.0))
        pick_after = rounded(jnp.where(code == after_ref[:, :chunk], 1.0, 0.0))
        blocks = jnp.where(lane < length, part, jnp.zeros_like(part))
        heads = rounded(dot(part[:, :lanes], shift))
        return dot(pick, blocks) + dot(pick_after, heads)

    if chunk == 2 * half:
        samples = part_samples(jnp.concatenate([table_ref[...], got_ref[...]], axis=0), 0)
    else:
        samples = jnp.zeros((frames, width), f32)
        for ref, first in ((table_ref, 0), (got_ref, half)):
            samples = lax.fori_loop(
                0,
                half // chunk,
                lambda i, s: s + part_samples(ref[rows_at(i, chunk), :], i * chunk + first),
                samples,
            )
    samples_ref[...] = rounded(samples)
    head_ref[...] = rounded(samples[:tail_rows, :lanes])


def windows(samples, start, per_block, offset):
    inside = iota(samples.shape, 1) - hop * lax.rem(iota((samples.shape[0], 1), 0) + start, per_block)
    inside = inside - offset
    return jnp.where((inside >= 0) & (inside < hop), samples, jnp.zeros_like(samples))


def rows_at(step, count):
    return pl.ds(pl.multiple_of(step * count, count), count)


def zero_forward_body(
    per_block, samples_ref, ce_ref, co_ref, gains_ref,
    act_even, act_odd, scaled_even, scaled_odd, slope_even, slope_odd, spread_even, spread_odd,
):
    samples = samples_ref[...]
    for conv, offset, act, scaled_ref, slope_ref, spread_ref in (
        (ce_ref, 0, act_even, scaled_even, slope_even, spread_even),
        (co_ref, hop // 2, act_odd, scaled_odd, slope_odd, spread_odd),
    ):
        pre = dot(windows(samples, 0, per_block, offset), conv[...])
        scaled, spread, normed = norm_parts(pre, gains_ref[0:1, :], gains_ref[1:2, :])
        value, slope = gelu_parts(normed)
        act[...] = rounded(value)
        scaled_ref[...] = scaled
        slope_ref[...] = slope
        spread_ref[...] = jnp.broadcast_to(spread, spread_ref.shape)


def layers_body(
    length, split,
    samples_ref, after_ref, ce_ref, co_ref, gains_ref, act_even, act_odd, cotangent_ref, conv_one_ref,
    feats_ref, back_one, back_prev, back_tail, fix_patch, fix_scaled, fix_slope, fix_spread,
    small_ref, *rest,
):
    keep = jnp.where(lax.axis_index("seq") < lax.axis_size("seq") - 1, 1.0, 0.0)
    frames, width = feats_ref.shape
    span = samples_ref.shape[1]
    per_block = length // hop
    if split:
        *split_refs, grad_ref, wide, act_last, act_next = rest
    else:
        grad_ref, wide, act_last, act_next = rest

    last = frames - tail_rows
    row = iota((lanes, span), 0)
    shift = rounded(jnp.where((iota((lanes, span), 1) == row + length) & (row < hop), keep, 0.0))
    after = dot(after_ref[...], shift)[0:1, :]
    patch_last = samples_ref[pl.ds(last, tail_rows), :].astype(f32)
    patch_last = windows(rounded(patch_last + jnp.where(iota((tail_rows, 1), 0) >= tail_rows - 1, after, 0.0)), last, per_block, hop // 2)
    patch_extra = rounded(jnp.where(iota((tail_rows, 1), 0) == 0, after, 0.0))
    fix_patch[0:tail_rows, :] = patch_last
    fix_patch[tail_rows:, :] = patch_extra
    pre = jnp.concatenate([dot(patch_last, co_ref[...]), dot(patch_extra, ce_ref[...])], axis=0)
    scaled, spread, normed = norm_parts(pre, gains_ref[0:1, :], gains_ref[1:2, :])
    value, slope = gelu_parts(normed)
    fix_scaled[...] = scaled
    fix_slope[...] = slope
    fix_spread[...] = jnp.broadcast_to(spread, fix_spread.shape)
    act_last[0:last, :] = act_odd[0:last, :]
    act_last[last:, :] = rounded(value[:tail_rows])
    wide[0:frames, :] = act_even[...].astype(f32)
    wide[pl.ds(frames, 8), :] = value[tail_rows : tail_rows + 8] * keep
    act_next[...] = rounded(wide[pl.ds(1, frames), :])

    pre = (
        dot(act_even[...], conv_one_ref[0:width, :])
        + dot(act_last[...], conv_one_ref[width : 2 * width, :])
        + dot(act_next[...], conv_one_ref[2 * width :, :])
    )
    scaled, spread, normed = norm_parts(pre, gains_ref[2:3, :], gains_ref[3:4, :])
    value, slope = gelu_parts(normed)
    feats_ref[...] = rounded(value)
    inner = cotangent_ref[...].astype(f32) * slope
    back = norm_back(inner, gains_ref[2:3, :], scaled, spread)
    back_one[...] = rounded(back)
    wide[0:8, :] = jnp.zeros((8, width), f32)
    wide[pl.ds(8, frames), :] = back
    small_ref[0:1, :] = jnp.sum(inner * scaled, axis=0, keepdims=True)
    small_ref[1:2, :] = jnp.sum(inner, axis=0, keepdims=True)

    back_prev[...] = rounded(wide[pl.ds(7, frames), :])
    first = iota((tail_rows, 1), 0) == 0
    back_tail[...] = rounded(jnp.where(first, wide[pl.ds(frames + 7, 1), :] * keep, 0.0))
    back = back_one[...]
    grad_ref[0:width, :] = dot_rows(act_even[...], back).astype(grad_ref.dtype)
    grad_ref[width : 2 * width, :] = dot_rows(act_last[...], back).astype(grad_ref.dtype)
    grad_ref[2 * width :, :] = dot_rows(act_next[...], back).astype(grad_ref.dtype)
    if split:
        core, _, _ = chip_bits()
        share = grad_ref.shape[0] // 8
        for k in range(4):
            at = pl.ds(k * share, share)
            for side in range(2):
                sent_ref, keep_ref = split_refs[2 * side : 2 * side + 2]
                columns = slice(side * width // 2, (side + 1) * width // 2)
                keep_ref[at, :] = grad_ref[rows_at(2 * k + core, share), columns]
                sent_ref[at, :] = grad_ref[rows_at(2 * k + 1 - core, share), columns]


def zero_backward_body(
    length,
    samples_ref, fix_patch, conv_one_ref, gains_ref, back_one, back_prev, back_tail,
    scaled_even, scaled_odd, slope_even, slope_odd, spread_even, spread_odd,
    fix_scaled, fix_slope, fix_spread, small_one,
    *rest,
):
    small_ref = rest[0] if len(rest) == 1 else rest[1]
    frames, width = back_one.shape
    span = samples_ref.shape[1]
    per_block = length // hop
    gain = gains_ref[0:1, :]
    last = frames - tail_rows
    back = back_one[...]
    third = conv_one_ref[2 * width :, :]
    up_even = dot_lanes(back, conv_one_ref[0:width, :]) + dot_lanes(back_prev[...], third)
    up_odd = dot_lanes(back, conv_one_ref[width : 2 * width, :])
    up_fix = jnp.concatenate([up_odd[last:], dot_lanes(back_tail[...], third)], axis=0)
    gain_sum, bias_sum, parts = 0.0, 0.0, []
    for up, scaled, slope, spread in (
        (up_even, scaled_even[...], slope_even[...], spread_even[:, 0:1]),
        (up_odd[:last], scaled_odd[0:last, :], slope_odd[0:last, :], spread_odd[0:last, 0:1]),
        (up_fix, fix_scaled[...], fix_slope[...], fix_spread[:, 0:1]),
    ):
        inner = up * slope
        back = norm_back(inner, gain, scaled, spread)
        high = rounded(back)
        parts.append((high, rounded(back - high.astype(f32))))
        gain_sum = gain_sum + jnp.sum(inner * scaled, axis=0, keepdims=True)
        bias_sum = bias_sum + jnp.sum(inner, axis=0, keepdims=True)

    tap = iota((span, lanes), 1)
    place = iota((span, lanes), 0)
    pick_even = rounded(jnp.where(lax.rem(place, hop) == tap, 1.0, 0.0))
    pick_odd = rounded(jnp.where(lax.rem(place + hop // 2, hop) == tap, 1.0, 0.0))
    samples = samples_ref[...]
    taps_even = rounded(dot(windows(samples, 0, per_block, 0), pick_even))
    taps_odd = rounded(dot(windows(samples, 0, per_block, hop // 2), pick_odd))
    taps_last = rounded(dot(fix_patch[0:tail_rows, :], pick_odd))
    taps_extra = rounded(dot(fix_patch[tail_rows:, :], pick_even))
    taps_fix = jnp.concatenate([taps_last, taps_extra], axis=0)
    grad = 0.0
    for taps, pair in zip((taps_even, taps_odd[:last], taps_fix), parts):
        for part in pair:
            grad = grad + dot_rows(taps, part)
    small_ref[...] = jnp.zeros(small_ref.shape, f32)
    small_ref[0:hop, :] = grad[0:hop, :]
    small_ref[hop : hop + 1, :] = gain_sum
    small_ref[hop + 1 : hop + 2, :] = bias_sum
    small_ref[hop + 2 : hop + 4, :] = small_one[0:2, :]
    if len(rest) > 1:
        sent_ref, _, out_ref = rest
        count = sent_ref.shape[0]
        out_ref[0:count, :] = sent_ref[...]
        store_small(out_ref, count, small_ref[...])


def prepare(conv_zero, place, gains, frames, span, per_block):
    width = conv_zero.shape[1]
    vectors = [g[None] for g in gains]
    scratch = [
        pltpu.VMEM(conv_zero.shape, bf16),
        pltpu.VMEM(place.shape, place.dtype),
        *[pltpu.VMEM(v.shape, f32) for v in vectors],
        pltpu.SemaphoreType.DMA((6,)),
    ]
    return call(
        functools.partial(prepare_body, per_block),
        [((span, width), bf16)] * 2 + [((frames, lanes), f32)] * 2 + [((8, width), f32)],
        conv_zero, place, *vectors,
        scratch=scratch,
        spaces=[pltpu.HBM] * 6,
    )


def run_layers(table, got, prepared, cotangent, conv_one, rows, length, capacity, split):
    frames, width = cotangent.shape
    span = table.shape[1]
    per_block = length // hop
    whole, half = ((frames, width), f32), ((frames, width), bf16)
    tail = 2 * tail_rows
    conv_even, conv_odd, place_rows, after_rows, gains = prepared
    samples, head = call(
        functools.partial(assemble_body, rows, length, capacity),
        [((frames, span), bf16), ((tail_rows, lanes), bf16)],
        table, got, place_rows, after_rows,
    )
    count = lax.axis_size("seq")
    after = lax.ppermute(head, "seq", [(i + 1, i) for i in range(count - 1)])
    act_even, act_odd, *saved = call(
        functools.partial(zero_forward_body, per_block),
        [half] * 2 + [whole] * 4 + [((frames, lanes), f32)] * 2,
        samples, conv_even, conv_odd, gains,
        flops=4 * 10**9,
    )
    outs = [half] * 3 + [
        ((tail_rows, width), bf16),
        ((tail, span), bf16),
        ((tail, width), f32),
        ((tail, width), f32),
        ((tail, lanes), f32),
        ((8, width), f32),
    ]
    grad = (3 * width, width)
    scratch = [
        pltpu.VMEM((frames + 16, width), f32),
        pltpu.VMEM(*half),
        pltpu.VMEM(*half),
    ]
    if split:
        outs += [((3 * width // 2, width // 2), bf16)] * 4
        scratch = [pltpu.VMEM(grad, bf16)] + scratch
    else:
        outs += [(grad, f32)]
    feats, back_one, back_prev, back_tail, fix_patch, *others = call(
        functools.partial(layers_body, length, split),
        outs,
        samples, after, conv_even, conv_odd, gains, act_even, act_odd, cotangent, conv_one,
        scratch=scratch,
        flops=6 * 10**9,
    )
    fix, small_one, grads = others[:3], others[3], others[4:]

    def backward(sent=None):
        outs, more = [((small_rows, width), f32)], []
        if sent is not None:
            outs.append(((sent.shape[0] + 4 * small_rows, sent.shape[1]), bf16))
            more.append(sent)
        return call(
            functools.partial(zero_backward_body, length),
            outs,
            samples, fix_patch, conv_one, gains, back_one, back_prev, back_tail,
            *saved, *fix, small_one, *more,
            flops=4 * 10**9,
        )

    return feats, grads, backward


def wide_split(small):
    high = rounded(small)
    return high, rounded(small - high.astype(f32))


def store_small(ref, start, small):
    width = ref.shape[1]
    for column in range(0, small.shape[1], width):
        for part in wide_split(small):
            ref[pl.ds(start, small_rows), :] = part[:, column : column + width]
            start += small_rows


def add_small(ref, start, small):
    width = ref.shape[1]
    columns = []
    for _ in range(0, small.shape[1], width):
        high, low = ref[pl.ds(start, small_rows), :], ref[pl.ds(start + small_rows, small_rows), :]
        columns.append(high.astype(f32) + low.astype(f32))
        start += 2 * small_rows
    high, low = wide_split(small)
    return (high.astype(f32) + low.astype(f32)) + jnp.concatenate(columns, axis=1)


def pass_small(got_ref, got_start, small_ref, sent_ref, sent_start, small_out):
    small = add_small(got_ref, got_start, small_ref[...])
    small_out[...] = small
    store_small(sent_ref, sent_start, small)


def chip_bits():
    spot = lax.axis_index("dp")
    return spot & 1, (spot >> 1) & 1, (spot >> 2) & 1


def core_body(left, keep_ref, got_ref, *refs):
    _, near, far = chip_bits()
    if left:
        sent_ref, kept_ref = refs
    else:
        small_ref, sent_ref, kept_ref, small_out = refs
    share = keep_ref.shape[0] // 4

    def total(k, mine):
        at = rows_at(2 * mine + k if left else 2 * k + mine, share)
        return keep_ref[at, :].astype(f32) + got_ref[at, :].astype(f32)

    mine = far if left else near
    for k in range(2):
        at = pl.ds(k * share, share)
        sent_ref[at, :] = rounded(total(k, 1 - mine))
        kept_ref[at, :] = total(k, mine)
    if not left:
        pass_small(got_ref, 4 * share, small_ref, sent_ref, 2 * share, small_out)


def chip_body(left, kept_ref, got_ref, *refs):
    _, near, far = chip_bits()
    if left:
        sent_ref, out_ref = refs
    else:
        small_ref, sent_ref, out_ref, small_out = refs
    share = out_ref.shape[0]
    mine = near if left else far

    def total(index):
        at = rows_at(index, share)
        return kept_ref[at, :] + got_ref[at, :].astype(f32)

    sent_ref[0:share, :] = rounded(total(1 - mine))
    out_ref[...] = total(mine)
    if not left:
        pass_small(got_ref, 2 * share, small_ref, sent_ref, share, small_out)


def time_body(left, kept_ref, got_ref, *refs):
    if left:
        (sent_ref,) = refs
    else:
        small_ref, sent_ref, small_out = refs
    share = sent_ref.shape[0] - (0 if left else 4 * small_rows)
    at = pl.ds(0, share)
    sent_ref[at, :] = rounded(kept_ref[at, :].astype(f32) + got_ref[at, :].astype(f32))
    if not left:
        pass_small(got_ref, share, small_ref, sent_ref, share, small_out)


def left_body(kept_ref, got_ref, out_ref):
    out_ref[...] = kept_ref[...].astype(f32) + got_ref[...].astype(f32)


def last_body(left_ref, kr_ref, gr_ref, small_ref, grad_ref, conv_ref, *vector_refs):
    share, half = left_ref.shape
    at = pl.ds(0, share)
    grad_ref[:, :half] = left_ref[...]
    grad_ref[:, half:] = kr_ref[at, :].astype(f32) + gr_ref[at, :].astype(f32)
    small = add_small(gr_ref, share, small_ref[...])
    conv_ref[...] = small[0:hop]
    for k, ref in enumerate(vector_refs):
        ref[...] = small[hop + k : hop + k + 1]


def sum_over_block(grads, backward):
    sent_left, keep_left, sent_right, keep_right = grads
    share, half = keep_left.shape[0] // 4, keep_left.shape[1]
    tail = 4 * small_rows
    kept_small = ((small_rows, 2 * half), f32)

    def kind(count, left, dtype=bf16):
        return ((count * share + (0 if left else tail), half), dtype)

    def stage(body, left, count, *args, behind=None):
        outs = [kind(count, left)]
        if body is not time_body:
            outs.append(kind(count, True, f32))
        if not left:
            outs.append(kept_small)
        return call(functools.partial(body, left), outs, *args, behind=behind, flops=6 * 10**8)

    got_left = swap(sent_left, 1)
    small, sent_right = backward(sent_right)
    got_right = swap(sent_right, 1)
    sl, kl = stage(core_body, True, 2, keep_left, got_left)
    gl = swap(sl, 4)
    sr, kr, small = stage(core_body, False, 2, keep_right, got_right, small, behind=kl)
    gr = swap(sr, 2)
    sl, kl = stage(chip_body, True, 1, kl, gl, behind=kr)
    gl = swap(sl, 2)
    sr, kr, small = stage(chip_body, False, 1, kr, gr, small, behind=kl)
    gr = swap(sr, 4)
    (sl,) = stage(time_body, True, 1, kl, gl, behind=kr)
    gl = swap_time(sl, 2)
    sr, small = stage(time_body, False, 1, kr, gr, small, behind=sl)
    gr = swap_time(sr, 1)
    (sl,) = stage(time_body, True, 1, sl, gl, behind=sr)
    gl = swap_time(sl, 1)
    sr, small = stage(time_body, False, 1, sr, gr, small, behind=sl)
    gr = swap_time(sr, 2)
    outs = [((share, 2 * half), f32), ((hop, 2 * half), f32)] + [((1, 2 * half), f32)] * 4
    (left,) = call(left_body, [kind(1, True, f32)], sl, gl, flops=6 * 10**8)
    grad, conv, *vectors = call(last_body, outs, left, sr, gr, small)
    return grad, conv, [v.reshape(-1) for v in vectors]


def on_device(
    audio_blocks,
    send_list,
    place_list,
    cotangent,
    conv_zero,
    conv_one,
    gain_zero,
    bias_zero,
    gain_one,
    bias_one,
):
    n_data, n_time = lax.axis_size("dp"), lax.axis_size("seq")
    blocks = audio_blocks[0]
    rows, length = blocks.shape
    capacity = send_list.shape[2] // n_data
    small_block = n_data == 8 and n_time == 4
    table, got = gather_blocks(blocks, send_list[0])
    gains = (gain_zero, bias_zero, gain_one, bias_one)
    prepared = prepare(
        conv_zero, place_list[0], gains, cotangent.shape[1], table.shape[1], length // hop
    )
    feats, grads, backward = run_layers(
        table, got, prepared, cotangent[0], conv_one, rows, length, capacity, small_block
    )
    if small_block:
        grad, conv, vectors = sum_over_block(grads, backward)
    else:
        grad = lax.psum_scatter(grads[0], "dp", scatter_dimension=0, tiled=True)
        grad = lax.psum(grad, "seq")
        small = lax.psum(backward()[0], ("dp", "seq"))
        conv, vectors = small[0:hop], [small[hop + k] for k in range(4)]
    return (feats[None], grad, conv, *vectors)


def solution(mesh):
    placed = (
        P("dp", "seq", None),
        P("seq", "dp", None),
        P("seq", "dp", None),
        P("dp", "seq", None),
        P(),
        P(),
        P(),
        P(),
        P(),
        P(),
    )
    return jax.shard_map(
        on_device,
        mesh=mesh,
        in_specs=placed,
        out_specs=(P("dp", "seq", None), P("dp", None), P(), P(), P(), P(), P()),
        check_vma=False,
    )
```

```python
import functools

import jax
import jax.numpy as jnp
from jax import lax
from jax.experimental import pallas as pl
from jax.experimental.pallas import tpu as pltpu
from jax.sharding import PartitionSpec as P

norm_eps = 1e-05
f32 = jnp.float32
bf16 = jnp.bfloat16
tail_rows = 16
small_rows = 16
lanes = 128
hop = 10


def dot(a, b):
    return jnp.dot(a, b, preferred_element_type=f32)


def dot_rows(a, b):
    return lax.dot_general(a, b, (((0,), (0,)), ((), ())), preferred_element_type=f32)


def dot_lanes(a, b):
    return lax.dot_general(a, b, (((1,), (1,)), ((), ())), preferred_element_type=f32)


def iota(shape, dim):
    return lax.broadcasted_iota(jnp.int32, shape, dim)


def rounded(value):
    return value.astype(bf16)


def row_mean(value):
    return jnp.mean(value, axis=-1, keepdims=True)


def norm_parts(pre_act, gain, bias):
    center = pre_act - row_mean(pre_act)
    spread = lax.rsqrt(row_mean(center * center) + norm_eps)
    scaled = center * spread
    return scaled, spread, scaled * gain + bias


def gelu_parts(normed):
    cdf = 0.5 + 0.5 * lax.erf(normed * 0.7071067811865476)
    density = jnp.exp2(normed * normed * -0.7213475204444817) * 0.3989422804014327
    return normed * cdf, cdf + normed * density


def norm_back(inner, gain, scaled, spread):
    pushed = inner * gain
    return spread * (pushed - row_mean(pushed) - scaled * row_mean(pushed * scaled))


def call(body, outs, *args, scratch=(), spaces=None, flops=0, behind=None):
    spaces = spaces or [pltpu.VMEM] * len(args)
    args = [
        pltpu.with_memory_space_constraint(a, pltpu.HBM) if space == pltpu.HBM else a
        for a, space in zip(args, spaces)
    ]
    size = sum(a.size * a.dtype.itemsize for a in args)
    count = len(args)
    run = body
    if behind is not None:
        args, spaces = [*args, behind], [*spaces, pl.ANY]

        def run(*refs):
            body(*refs[:count], *refs[count + 1 :])

    return pl.pallas_call(
        run,
        out_shape=[jax.ShapeDtypeStruct(s, t) for s, t in outs],
        in_specs=[pl.BlockSpec(memory_space=space) for space in spaces],
        out_specs=[pl.BlockSpec(memory_space=pltpu.VMEM)] * len(outs),
        scratch_shapes=list(scratch),
        compiler_params=pltpu.CompilerParams(vmem_limit_bytes=40 << 20),
        cost_estimate=pl.CostEstimate(flops=flops, bytes_accessed=size, transcendentals=0),
    )(*args)


def swap(value, mask):
    count = lax.axis_size("dp")
    return lax.ppermute(value, "dp", [(i, i ^ mask) for i in range(count)])


def swap_time(value, mask):
    count = lax.axis_size("seq")
    return lax.ppermute(value, "seq", [(i, i ^ mask) for i in range(count)])


def packed(blocks, sends, width):
    rows, length = blocks.shape
    slots = sends.shape[1]
    hit = sends == iota((rows, slots), 0)
    spot = jnp.sum(jnp.where(hit, iota((rows, slots), 1).astype(f32), 0.0), axis=1, keepdims=True)
    blocks = jnp.concatenate([blocks.astype(f32), jnp.zeros((rows, width - length), f32)], axis=1)
    return rounded(jnp.where(iota((rows, width), 1) == length, spot, blocks))


def pack_body(blocks_ref, sends_ref, own_ref, blocks_here, sends_here, sems):
    fetch((blocks_ref, sends_ref), (blocks_here, sends_here), sems)
    own_ref[...] = packed(blocks_here[...], sends_here[...], own_ref.shape[1])


def pair_body(own_ref, blocks_ref, sends_ref, out_ref):
    rows, width = own_ref.shape
    out_ref[0:rows, :] = own_ref[...]
    out_ref[rows:, :] = packed(blocks_ref[...], sends_ref[...], width)


def join_body(a_ref, b_ref, out_ref):
    out_ref[...] = jnp.concatenate([a_ref[...], b_ref[...]], axis=0)


def gather_blocks(blocks, sends):
    rows, length = blocks.shape
    width = -(-(length + hop) // lanes) * lanes
    scratch = [
        pltpu.VMEM(blocks.shape, bf16),
        pltpu.VMEM(sends.shape, sends.dtype),
        pltpu.SemaphoreType.DMA((2,)),
    ]
    (table,) = call(
        pack_body, [((rows, width), bf16)], blocks, sends, scratch=scratch, spaces=[pltpu.HBM] * 2
    )
    (table,) = call(
        pair_body, [((2 * rows, width), bf16)], table, swap(blocks, 1), swap(sends, 1)
    )
    count = lax.axis_size("dp")
    if count == 8:
        return [table, *(swap(table, mask) for mask in (3, 5, 7))]
    step = 2
    while step < count:
        got = swap(table, step | 1)
        step *= 2
        (table,) = call(join_body, [((rows * step, width), bf16)], table, got)
    return [table]


def fetch(refs, buffers, sems):
    copies = [pltpu.make_async_copy(r, b, sems.at[k]) for k, (r, b) in enumerate(zip(refs, buffers))]
    for copy in copies:
        copy.start()
    for copy in copies:
        copy.wait()


def prepare_body(
    per_block,
    conv_hbm, place_hbm, *refs,
):
    vectors, (even_ref, odd_ref, place_ref, after_ref, gains_ref) = refs[:4], refs[4:9]
    conv_here, place_here, *vectors_here, sems = refs[9:]
    fetch((conv_hbm, place_hbm, *vectors), (conv_here, place_here, *vectors_here), sems)
    width = even_ref.shape[0]
    taps = conv_here.shape[0]
    conv = conv_here[...]
    for ref, offset in ((even_ref, 0), (odd_ref, hop // 2)):
        spot = iota((width, taps), 0) + offset
        ref[...] = rounded(
            dot(rounded(jnp.where(lax.rem(spot, hop) == iota((width, taps), 1), 1.0, 0.0)), conv)
        )
    frames = place_ref.shape[0]
    rows = place_here.shape[1]
    place = rounded(jnp.broadcast_to(place_here[...].astype(f32), (lanes, rows)))
    block = lax.div(iota((frames, rows), 0), per_block)
    for ref, offset in ((place_ref, 0), (after_ref, 1)):
        wanted = dot_lanes(rounded(jnp.where(block + offset == iota((frames, rows), 1), 1.0, 0.0)), place)
        ref[...] = jnp.where(iota((frames, 1), 0) + offset * per_block < frames, wanted, -2.0)
    gains_ref[...] = jnp.concatenate([v[...] for v in vectors_here] * 2, axis=0)


def assemble_body(rows, length, capacity, place_ref, after_ref, *refs):
    here = lax.axis_index("dp")
    *table_refs, samples_ref, head_ref = refs
    frames, width = samples_ref.shape
    total = sum(ref.shape[0] for ref in table_refs)
    chunk = min(total, lanes)
    row = iota((lanes, width), 0)
    shift = rounded(jnp.where((iota((lanes, width), 1) == row + length) & (row < hop), 1.0, 0.0))
    mark = rounded(jnp.where(iota((tail_rows, width), 1) == length, 1.0, 0.0))
    lane = iota((chunk, width), 1)
    low = here * capacity

    def part_samples(part, first):
        spot = dot_lanes(mark, part)[0:1, :].astype(jnp.int32)
        slot = lax.div(iota((1, chunk), 1) + first, rows)
        source, bits = slot ^ here, 2
        if len(table_refs) > 1:
            source = source ^ jnp.where(slot >= 2, 1, 0)
        while len(table_refs) == 1 and bits < total // rows:
            source = source ^ jnp.where((slot & bits) != 0, 1, 0)
            bits *= 2
        mine = (spot >= low) & (spot < low + capacity)
        code = jnp.where(mine, source * capacity + spot - low, -1).astype(f32)
        pick = rounded(jnp.where(code == place_ref[:, :chunk], 1.0, 0.0))
        pick_after = rounded(jnp.where(code == after_ref[:, :chunk], 1.0, 0.0))
        blocks = jnp.where(lane < length, part, jnp.zeros_like(part))
        heads = rounded(dot(part[:, :lanes], shift))
        return dot(pick, blocks) + dot(pick_after, heads)

    if total == chunk:
        samples = part_samples(jnp.concatenate([ref[...] for ref in table_refs], axis=0), 0)
    else:
        (table_ref,) = table_refs
        samples = lax.fori_loop(
            0,
            total // chunk,
            lambda i, s: s + part_samples(table_ref[rows_at(i, chunk), :], i * chunk),
            jnp.zeros((frames, width), f32),
        )
    samples_ref[...] = rounded(samples)
    head_ref[...] = rounded(samples[:tail_rows, :lanes])


def windows(samples, start, per_block, offset):
    inside = iota(samples.shape, 1) - hop * lax.rem(iota((samples.shape[0], 1), 0) + start, per_block)
    inside = inside - offset
    return jnp.where((inside >= 0) & (inside < hop), samples, jnp.zeros_like(samples))


def rows_at(step, count):
    return pl.ds(pl.multiple_of(step * count, count), count)


def zero_forward_body(
    per_block, samples_ref, ce_ref, co_ref, gains_ref,
    act_even, act_odd, scaled_even, scaled_odd, slope_even, slope_odd, spread_even, spread_odd,
):
    samples = samples_ref[...]
    for conv, offset, act, scaled_ref, slope_ref, spread_ref in (
        (ce_ref, 0, act_even, scaled_even, slope_even, spread_even),
        (co_ref, hop // 2, act_odd, scaled_odd, slope_odd, spread_odd),
    ):
        pre = dot(windows(samples, 0, per_block, offset), conv[...])
        scaled, spread, normed = norm_parts(pre, gains_ref[0:1, :], gains_ref[1:2, :])
        value, slope = gelu_parts(normed)
        act[...] = rounded(value)
        scaled_ref[...] = scaled
        slope_ref[...] = slope
        spread_ref[...] = jnp.broadcast_to(spread, spread_ref.shape)


def layers_body(
    length, split,
    samples_ref, after_ref, ce_ref, co_ref, gains_ref, act_even, act_odd, cotangent_ref, conv_one_ref,
    feats_ref, back_one, back_prev, back_tail, fix_patch, fix_scaled, fix_slope, fix_spread,
    small_ref, *rest,
):
    keep = jnp.where(lax.axis_index("seq") < lax.axis_size("seq") - 1, 1.0, 0.0)
    frames, width = feats_ref.shape
    span = samples_ref.shape[1]
    per_block = length // hop
    if split:
        *split_refs, grad_ref, wide, act_last, act_next = rest
    else:
        grad_ref, wide, act_last, act_next = rest

    last = frames - tail_rows
    row = iota((lanes, span), 0)
    shift = rounded(jnp.where((iota((lanes, span), 1) == row + length) & (row < hop), keep, 0.0))
    after = dot(after_ref[...], shift)[0:1, :]
    patch_last = samples_ref[pl.ds(last, tail_rows), :].astype(f32)
    patch_last = windows(rounded(patch_last + jnp.where(iota((tail_rows, 1), 0) >= tail_rows - 1, after, 0.0)), last, per_block, hop // 2)
    patch_extra = rounded(jnp.where(iota((tail_rows, 1), 0) == 0, after, 0.0))
    fix_patch[0:tail_rows, :] = patch_last
    fix_patch[tail_rows:, :] = patch_extra
    pre = jnp.concatenate([dot(patch_last, co_ref[...]), dot(patch_extra, ce_ref[...])], axis=0)
    scaled, spread, normed = norm_parts(pre, gains_ref[0:1, :], gains_ref[1:2, :])
    value, slope = gelu_parts(normed)
    fix_scaled[...] = scaled
    fix_slope[...] = slope
    fix_spread[...] = jnp.broadcast_to(spread, fix_spread.shape)
    act_last[0:last, :] = act_odd[0:last, :]
    act_last[last:, :] = rounded(value[:tail_rows])
    wide[0:frames, :] = act_even[...].astype(f32)
    wide[pl.ds(frames, 8), :] = value[tail_rows : tail_rows + 8] * keep
    act_next[...] = rounded(wide[pl.ds(1, frames), :])

    wide[0:8, :] = jnp.zeros((8, width), f32)
    gain_sum, bias_sum = 0.0, 0.0
    count = frames // 4
    parts = [pl.ds(k * count, count) for k in range(4)]
    pre_parts = [
        dot(act_even[at, :], conv_one_ref[0:width, :])
        + dot(act_last[at, :], conv_one_ref[width : 2 * width, :])
        + dot(act_next[at, :], conv_one_ref[2 * width :, :])
        for at in parts
    ]
    for k, (at, pre) in enumerate(zip(parts, pre_parts)):
        scaled, spread, normed = norm_parts(pre, gains_ref[2:3, :], gains_ref[3:4, :])
        value, slope = gelu_parts(normed)
        feats_ref[at, :] = rounded(value)
        inner = cotangent_ref[at, :].astype(f32) * slope
        back = norm_back(inner, gains_ref[2:3, :], scaled, spread)
        back_one[at, :] = rounded(back)
        wide[pl.ds(8 + k * count, count), :] = back
        gain_sum = gain_sum + jnp.sum(inner * scaled, axis=0, keepdims=True)
        bias_sum = bias_sum + jnp.sum(inner, axis=0, keepdims=True)
    small_ref[0:1, :] = gain_sum
    small_ref[1:2, :] = bias_sum

    back_prev[...] = rounded(wide[pl.ds(7, frames), :])
    first = iota((tail_rows, 1), 0) == 0
    back_tail[...] = rounded(jnp.where(first, wide[pl.ds(frames + 7, 1), :] * keep, 0.0))
    back = back_one[...]
    grad_ref[0:width, :] = dot_rows(act_even[...], back).astype(grad_ref.dtype)
    grad_ref[width : 2 * width, :] = dot_rows(act_last[...], back).astype(grad_ref.dtype)
    grad_ref[2 * width :, :] = dot_rows(act_next[...], back).astype(grad_ref.dtype)
    if split:
        core, _, _ = chip_bits()
        share = grad_ref.shape[0] // 8
        start = 0
        for side in range(2):
            sent_ref, keep_ref = split_refs[2 * side : 2 * side + 2]
            count = keep_ref.shape[0] // 4
            for k in range(4):
                at = pl.ds(k * count, count)
                for ref, index in ((keep_ref, 2 * k + core), (sent_ref, 2 * k + 1 - core)):
                    ref[at, :] = grad_ref[pl.ds(pl.multiple_of(index * share + start, 16), count), :]
            start += count


def zero_backward_body(
    length,
    samples_ref, fix_patch, conv_one_ref, gains_ref, back_one, back_prev, back_tail,
    scaled_even, scaled_odd, slope_even, slope_odd, spread_even, spread_odd,
    fix_scaled, fix_slope, fix_spread, small_one,
    *rest,
):
    small_ref = rest[0] if len(rest) == 1 else rest[1]
    frames, width = back_one.shape
    span = samples_ref.shape[1]
    per_block = length // hop
    gain = gains_ref[0:1, :]
    last = frames - tail_rows
    back = back_one[...]
    third = conv_one_ref[2 * width :, :]
    up_even = dot_lanes(back, conv_one_ref[0:width, :]) + dot_lanes(back_prev[...], third)
    up_odd = dot_lanes(back, conv_one_ref[width : 2 * width, :])
    up_fix = jnp.concatenate([up_odd[last:], dot_lanes(back_tail[...], third)], axis=0)
    gain_sum, bias_sum, parts = 0.0, 0.0, []
    for up, scaled, slope, spread in (
        (up_even, scaled_even[...], slope_even[...], spread_even[:, 0:1]),
        (up_odd[:last], scaled_odd[0:last, :], slope_odd[0:last, :], spread_odd[0:last, 0:1]),
        (up_fix, fix_scaled[...], fix_slope[...], fix_spread[:, 0:1]),
    ):
        inner = up * slope
        back = norm_back(inner, gain, scaled, spread)
        high = rounded(back)
        parts.append((high, rounded(back - high.astype(f32))))
        gain_sum = gain_sum + jnp.sum(inner * scaled, axis=0, keepdims=True)
        bias_sum = bias_sum + jnp.sum(inner, axis=0, keepdims=True)

    tap = iota((span, lanes), 1)
    place = iota((span, lanes), 0)
    pick_even = rounded(jnp.where(lax.rem(place, hop) == tap, 1.0, 0.0))
    pick_odd = rounded(jnp.where(lax.rem(place + hop // 2, hop) == tap, 1.0, 0.0))
    samples = samples_ref[...]
    taps_even = rounded(dot(windows(samples, 0, per_block, 0), pick_even))
    taps_odd = rounded(dot(windows(samples, 0, per_block, hop // 2), pick_odd))
    taps_last = rounded(dot(fix_patch[0:tail_rows, :], pick_odd))
    taps_extra = rounded(dot(fix_patch[tail_rows:, :], pick_even))
    taps_fix = jnp.concatenate([taps_last, taps_extra], axis=0)
    grad = 0.0
    for taps, pair in zip((taps_even, taps_odd[:last], taps_fix), parts):
        for part in pair:
            grad = grad + dot_rows(taps, part)
    small_ref[...] = jnp.zeros(small_ref.shape, f32)
    small_ref[0:hop, :] = grad[0:hop, :]
    small_ref[hop : hop + 1, :] = gain_sum
    small_ref[hop + 1 : hop + 2, :] = bias_sum
    small_ref[hop + 2 : hop + 4, :] = small_one[0:2, :]
    if len(rest) > 1:
        sent_ref, _, out_ref = rest
        count = sent_ref.shape[0]
        out_ref[0:count, :] = sent_ref[...]
        store_small(out_ref, count, small_ref[...])


def prepare(conv_zero, place, gains, frames, span, per_block):
    width = conv_zero.shape[1]
    vectors = [g[None] for g in gains]
    scratch = [
        pltpu.VMEM(conv_zero.shape, bf16),
        pltpu.VMEM(place.shape, place.dtype),
        *[pltpu.VMEM(v.shape, f32) for v in vectors],
        pltpu.SemaphoreType.DMA((6,)),
    ]
    return call(
        functools.partial(prepare_body, per_block),
        [((span, width), bf16)] * 2 + [((frames, lanes), f32)] * 2 + [((8, width), f32)],
        conv_zero, place, *vectors,
        scratch=scratch,
        spaces=[pltpu.HBM] * 6,
    )


def run_layers(tables, prepared, cotangent, conv_one, rows, length, capacity, split):
    frames, width = cotangent.shape
    span = tables[0].shape[1]
    per_block = length // hop
    whole, half = ((frames, width), f32), ((frames, width), bf16)
    tail = 2 * tail_rows
    conv_even, conv_odd, place_rows, after_rows, gains = prepared
    samples, head = call(
        functools.partial(assemble_body, rows, length, capacity),
        [((frames, span), bf16), ((tail_rows, lanes), bf16)],
        place_rows, after_rows, *tables,
    )
    count = lax.axis_size("seq")
    after = lax.ppermute(head, "seq", [(i + 1, i) for i in range(count - 1)])
    act_even, act_odd, *saved = call(
        functools.partial(zero_forward_body, per_block),
        [half] * 2 + [whole] * 4 + [((frames, lanes), f32)] * 2,
        samples, conv_even, conv_odd, gains,
        flops=4 * 10**9,
    )
    outs = [half] * 3 + [
        ((tail_rows, width), bf16),
        ((tail, span), bf16),
        ((tail, width), f32),
        ((tail, width), f32),
        ((tail, lanes), f32),
        ((8, width), f32),
    ]
    grad = (3 * width, width)
    scratch = [
        pltpu.VMEM((frames + 16, width), f32),
        pltpu.VMEM(*half),
        pltpu.VMEM(*half),
    ]
    if split:
        for count in share_parts(3 * width // 8):
            outs += [((4 * count, width), bf16)] * 2
        scratch = [pltpu.VMEM(grad, bf16)] + scratch
    else:
        outs += [(grad, f32)]
    feats, back_one, back_prev, back_tail, fix_patch, *others = call(
        functools.partial(layers_body, length, split),
        outs,
        samples, after, conv_even, conv_odd, gains, act_even, act_odd, cotangent, conv_one,
        scratch=scratch,
        flops=6 * 10**9,
    )
    fix, small_one, grads = others[:3], others[3], others[4:]

    def backward(sent=None):
        outs, more = [((small_rows, width), f32)], []
        if sent is not None:
            outs.append(((sent.shape[0] + 2 * small_rows, sent.shape[1]), bf16))
            more.append(sent)
        return call(
            functools.partial(zero_backward_body, length),
            outs,
            samples, fix_patch, conv_one, gains, back_one, back_prev, back_tail,
            *saved, *fix, small_one, *more,
            flops=4 * 10**9,
        )

    return feats, grads, backward


def share_parts(share):
    left = 32 * (share // 48)
    return left, share - left


def wide_split(small):
    high = rounded(small)
    return high, rounded(small - high.astype(f32))


def store_small(ref, start, small, parts=2):
    for k, part in enumerate(wide_split(small)[:parts]):
        ref[pl.ds(start + k * small_rows, small_rows), :] = part


def add_small(ref, start, small, parts=2):
    for k, part in enumerate(wide_split(small)[:parts]):
        part = part.astype(f32)
        other = ref[pl.ds(start + k * small_rows, small_rows), :].astype(f32)
        total = part + other if k == 0 else total + (part + other)
    return total


def pass_small(got_ref, got_start, small_ref, sent_ref, sent_start, small_out, got=2, sent=2):
    small = add_small(got_ref, got_start, small_ref[...], got)
    small_out[...] = small
    store_small(sent_ref, sent_start, small, sent)


def chip_bits():
    spot = lax.axis_index("dp")
    return spot & 1, (spot >> 1) & 1, (spot >> 2) & 1


def core_body(left, keep_ref, got_ref, *refs):
    _, near, far = chip_bits()
    if left:
        sent_ref, kept_ref = refs
    else:
        small_ref, sent_ref, kept_ref, small_out = refs
    share = keep_ref.shape[0] // 4

    def total(k, mine):
        at = rows_at(2 * mine + k if left else 2 * k + mine, share)
        return keep_ref[at, :].astype(f32) + got_ref[at, :].astype(f32)

    mine = far if left else near
    for k in range(2):
        at = pl.ds(k * share, share)
        sent_ref[at, :] = rounded(total(k, 1 - mine))
        kept_ref[at, :] = total(k, mine)
    if not left:
        pass_small(got_ref, 4 * share, small_ref, sent_ref, 2 * share, small_out)


def chip_body(left, kept_ref, got_ref, *refs):
    _, near, far = chip_bits()
    if left:
        sent_ref, out_ref = refs
    else:
        small_ref, sent_ref, out_ref, small_out = refs
    share = out_ref.shape[0]
    mine = near if left else far

    def total(index):
        at = rows_at(index, share)
        return kept_ref[at, :] + got_ref[at, :].astype(f32)

    sent_ref[0:share, :] = rounded(total(1 - mine))
    out_ref[...] = total(mine)
    if not left:
        pass_small(got_ref, 2 * share, small_ref, sent_ref, share, small_out)


def time_body(left, kept_ref, got_ref, *refs, got):
    if left:
        (sent_ref,) = refs
    else:
        small_ref, sent_ref, small_out = refs
    share = sent_ref.shape[0] - (0 if left else small_rows)
    at = pl.ds(0, share)
    sent_ref[at, :] = rounded(kept_ref[at, :].astype(f32) + got_ref[at, :].astype(f32))
    if not left:
        pass_small(got_ref, share, small_ref, sent_ref, share, small_out, got, 1)


def left_body(kept_ref, got_ref, out_ref):
    out_ref[...] = kept_ref[...].astype(f32) + got_ref[...].astype(f32)


def last_body(left_ref, kr_ref, gr_ref, small_ref, grad_ref, conv_ref, *vector_refs):
    left, right = share_parts(grad_ref.shape[0])
    at = pl.ds(0, right)
    grad_ref[0:left, :] = left_ref[...]
    grad_ref[left:, :] = kr_ref[at, :].astype(f32) + gr_ref[at, :].astype(f32)
    small = add_small(gr_ref, right, small_ref[...], 1)
    conv_ref[...] = small[0:hop]
    for k, ref in enumerate(vector_refs):
        ref[...] = small[hop + k : hop + k + 1]


def copy_body(a_ref, out_ref, token_ref):
    out_ref[...] = a_ref[...]
    token_ref[...] = jnp.zeros(token_ref.shape, f32)


def sum_over_block(feats, grads, backward):
    sent_left, keep_left, sent_right, keep_right = grads
    width = keep_left.shape[1]
    parts = keep_left.shape[0] // 4, keep_right.shape[0] // 4
    kept_small = ((small_rows, width), f32)

    first_step = functools.partial(time_body, got=2)
    later_step = functools.partial(time_body, got=1)

    def kind(count, left, dtype=bf16, tails=0):
        return ((count * parts[0 if left else 1] + small_rows * tails, width), dtype)

    def stage(body, left, count, *args, behind=None):
        along_chips = body in (core_body, chip_body)
        outs = [kind(count, left, tails=0 if left else 2 if along_chips else 1)]
        if along_chips:
            outs.append(kind(count, left, f32))
        if not left:
            outs.append(kept_small)
        run = functools.partial(body, left)
        return call(run, outs, *args, behind=behind, flops=6 * 10**8)

    got_left = swap(sent_left, 1)
    small, sent_right = backward(sent_right)
    got_right = swap(sent_right, 1)
    sl, kl = stage(core_body, True, 2, keep_left, got_left)
    gl = swap(sl, 4)
    sr, kr, small = stage(core_body, False, 2, keep_right, got_right, small, behind=kl)
    gr = swap(sr, 2)
    feats, token = call(copy_body, [(feats.shape, bf16), ((8, lanes), f32)], feats, behind=sr)
    sl, kl = stage(chip_body, True, 1, kl, gl, behind=token)
    gl = swap(sl, 2)
    sr, kr, small = stage(chip_body, False, 1, kr, gr, small, behind=kl)
    gr = swap(sr, 4)
    (sl,) = stage(first_step, True, 1, kl, gl, behind=kr)
    gl = swap_time(sl, 2)
    sr, small = stage(first_step, False, 1, kr, gr, small, behind=sl)
    gr = swap_time(sr, 1)
    (sl,) = stage(later_step, True, 1, sl, gl, behind=sr)
    gl = swap_time(sl, 1)
    sr, small = stage(later_step, False, 1, sr, gr, small, behind=sl)
    gr = swap_time(sr, 2)
    outs = [((sum(parts), width), f32), ((hop, width), f32)] + [((1, width), f32)] * 4
    (left,) = call(left_body, [kind(1, True, f32)], sl, gl, flops=6 * 10**8)
    grad, conv, *vectors = call(last_body, outs, left, sr, gr, small)
    return feats, grad, conv, [v.reshape(-1) for v in vectors]


def on_device(
    audio_blocks,
    send_list,
    place_list,
    cotangent,
    conv_zero,
    conv_one,
    gain_zero,
    bias_zero,
    gain_one,
    bias_one,
):
    n_data, n_time = lax.axis_size("dp"), lax.axis_size("seq")
    blocks = audio_blocks[0]
    rows, length = blocks.shape
    capacity = send_list.shape[2] // n_data
    small_block = n_data == 8 and n_time == 4
    tables = gather_blocks(blocks, send_list[0])
    gains = (gain_zero, bias_zero, gain_one, bias_one)
    prepared = prepare(
        conv_zero, place_list[0], gains, cotangent.shape[1], tables[0].shape[1], length // hop
    )
    feats, grads, backward = run_layers(
        tables, prepared, cotangent[0], conv_one, rows, length, capacity, small_block
    )
    if small_block:
        feats, grad, conv, vectors = sum_over_block(feats, grads, backward)
    else:
        grad = lax.psum_scatter(grads[0], "dp", scatter_dimension=0, tiled=True)
        grad = lax.psum(grad, "seq")
        small = lax.psum(backward()[0], ("dp", "seq"))
        conv, vectors = small[0:hop], [small[hop + k] for k in range(4)]
    return (feats[None], grad, conv, *vectors)


def solution(mesh):
    placed = (
        P("dp", "seq", None),
        P("seq", "dp", None),
        P("seq", "dp", None),
        P("dp", "seq", None),
        P(),
        P(),
        P(),
        P(),
        P(),
        P(),
    )
    return jax.shard_map(
        on_device,
        mesh=mesh,
        in_specs=placed,
        out_specs=(P("dp", "seq", None), P("dp", None), P(), P(), P(), P(), P()),
        check_vma=False,
    )
```

```python
import functools

import jax
import jax.numpy as jnp
from jax import lax
from jax.experimental import pallas as pl
from jax.experimental.pallas import tpu as pltpu
from jax.sharding import PartitionSpec as P

norm_eps = 1e-05
f32 = jnp.float32
bf16 = jnp.bfloat16
tail_rows = 16
small_rows = 16
lanes = 128
hop = 10


def dot(a, b):
    return jnp.dot(a, b, preferred_element_type=f32)


def dot_rows(a, b):
    return lax.dot_general(a, b, (((0,), (0,)), ((), ())), preferred_element_type=f32)


def dot_lanes(a, b):
    return lax.dot_general(a, b, (((1,), (1,)), ((), ())), preferred_element_type=f32)


def iota(shape, dim):
    return lax.broadcasted_iota(jnp.int32, shape, dim)


def rounded(value):
    return value.astype(bf16)


def row_mean(value):
    return jnp.mean(value, axis=-1, keepdims=True)


def norm_parts(pre_act, gain, bias):
    center = pre_act - row_mean(pre_act)
    spread = lax.rsqrt(row_mean(center * center) + norm_eps)
    scaled = center * spread
    return scaled, spread, scaled * gain + bias


def gelu_parts(normed):
    cdf = 0.5 + 0.5 * lax.erf(normed * 0.7071067811865476)
    density = jnp.exp2(normed * normed * -0.7213475204444817) * 0.3989422804014327
    return normed * cdf, cdf + normed * density


def norm_back(inner, gain, scaled, spread):
    pushed = inner * gain
    return spread * (pushed - row_mean(pushed) - scaled * row_mean(pushed * scaled))


def call(body, outs, *args, scratch=(), spaces=None, flops=0, behind=None):
    spaces = spaces or [pltpu.VMEM] * len(args)
    args = [
        pltpu.with_memory_space_constraint(a, pltpu.HBM) if space == pltpu.HBM else a
        for a, space in zip(args, spaces)
    ]
    size = sum(a.size * a.dtype.itemsize for a in args)
    count = len(args)
    run = body
    if behind is not None:
        args, spaces = [*args, behind], [*spaces, pl.ANY]

        def run(*refs):
            body(*refs[:count], *refs[count + 1 :])

    return pl.pallas_call(
        run,
        out_shape=[jax.ShapeDtypeStruct(s, t) for s, t in outs],
        in_specs=[pl.BlockSpec(memory_space=space) for space in spaces],
        out_specs=[pl.BlockSpec(memory_space=pltpu.VMEM)] * len(outs),
        scratch_shapes=list(scratch),
        compiler_params=pltpu.CompilerParams(vmem_limit_bytes=40 << 20),
        cost_estimate=pl.CostEstimate(flops=flops, bytes_accessed=size, transcendentals=0),
    )(*args)


def swap(value, mask):
    count = lax.axis_size("dp")
    return lax.ppermute(value, "dp", [(i, i ^ mask) for i in range(count)])


def swap_time(value, mask):
    count = lax.axis_size("seq")
    return lax.ppermute(value, "seq", [(i, i ^ mask) for i in range(count)])


def packed(blocks, sends, width):
    rows, length = blocks.shape
    slots = sends.shape[1]
    hit = sends == iota((rows, slots), 0)
    spot = jnp.sum(jnp.where(hit, iota((rows, slots), 1).astype(f32), 0.0), axis=1, keepdims=True)
    blocks = jnp.concatenate([blocks.astype(f32), jnp.zeros((rows, width - length), f32)], axis=1)
    return rounded(jnp.where(iota((rows, width), 1) == length, spot, blocks))


def pack_body(blocks_ref, sends_ref, own_ref, blocks_here, sends_here, sems):
    fetch((blocks_ref, sends_ref), (blocks_here, sends_here), sems)
    own_ref[...] = packed(blocks_here[...], sends_here[...], own_ref.shape[1])


def pair_body(own_ref, blocks_ref, sends_ref, out_ref):
    rows, width = own_ref.shape
    out_ref[0:rows, :] = own_ref[...]
    out_ref[rows:, :] = packed(blocks_ref[...], sends_ref[...], width)


def join_body(a_ref, b_ref, out_ref):
    out_ref[...] = jnp.concatenate([a_ref[...], b_ref[...]], axis=0)


def gather_blocks(blocks, sends):
    rows, length = blocks.shape
    width = -(-(length + hop) // lanes) * lanes
    scratch = [
        pltpu.VMEM(blocks.shape, bf16),
        pltpu.VMEM(sends.shape, sends.dtype),
        pltpu.SemaphoreType.DMA((2,)),
    ]
    (table,) = call(
        pack_body, [((rows, width), bf16)], blocks, sends, scratch=scratch, spaces=[pltpu.HBM] * 2
    )
    (table,) = call(
        pair_body, [((2 * rows, width), bf16)], table, swap(blocks, 1), swap(sends, 1)
    )
    count = lax.axis_size("dp")
    if count == 8:
        return [table, *(swap(table, mask) for mask in (3, 5, 7))]
    step = 2
    while step < count:
        got = swap(table, step | 1)
        step *= 2
        (table,) = call(join_body, [((rows * step, width), bf16)], table, got)
    return [table]


def fetch(refs, buffers, sems):
    copies = [pltpu.make_async_copy(r, b, sems.at[k]) for k, (r, b) in enumerate(zip(refs, buffers))]
    for copy in copies:
        copy.start()
    for copy in copies:
        copy.wait()


def prepare_body(
    per_block,
    conv_hbm, place_hbm, *refs,
):
    vectors, (even_ref, odd_ref, place_ref, after_ref, gains_ref) = refs[:4], refs[4:9]
    conv_here, place_here, *vectors_here, sems = refs[9:]
    fetch((conv_hbm, place_hbm, *vectors), (conv_here, place_here, *vectors_here), sems)
    width = even_ref.shape[0]
    taps = conv_here.shape[0]
    conv = conv_here[...]
    for ref, offset in ((even_ref, 0), (odd_ref, hop // 2)):
        spot = iota((width, taps), 0) + offset
        ref[...] = rounded(
            dot(rounded(jnp.where(lax.rem(spot, hop) == iota((width, taps), 1), 1.0, 0.0)), conv)
        )
    frames = place_ref.shape[0]
    rows = place_here.shape[1]
    place = rounded(jnp.broadcast_to(place_here[...].astype(f32), (lanes, rows)))
    block = lax.div(iota((frames, rows), 0), per_block)
    for ref, offset in ((place_ref, 0), (after_ref, 1)):
        wanted = dot_lanes(rounded(jnp.where(block + offset == iota((frames, rows), 1), 1.0, 0.0)), place)
        ref[...] = jnp.where(iota((frames, 1), 0) + offset * per_block < frames, wanted, -2.0)
    gains_ref[...] = jnp.concatenate([v[...] for v in vectors_here] * 2, axis=0)


def assembled(rows, length, capacity, table_refs, place, after, width):
    here = lax.axis_index("dp")
    total = sum(ref.shape[0] for ref in table_refs)
    chunk = min(total, lanes)
    frames = place.shape[0]
    place, low = place[:, :chunk], here * capacity
    mark = rounded(jnp.where(iota((tail_rows, table_refs[0].shape[1]), 1) == length, 1.0, 0.0))
    lane = iota((chunk, width), 1)
    if after is not None:
        after = after[:, :chunk]
        row = iota((lanes, width), 0)
        shift = rounded(jnp.where((iota((lanes, width), 1) == row + length) & (row < hop), 1.0, 0.0))

    def part_samples(part, first):
        spot = dot_lanes(mark, part)[0:1, :].astype(jnp.int32)
        slot = lax.div(iota((1, chunk), 1) + first, rows)
        source, bits = slot ^ here, 2
        if len(table_refs) > 1:
            source = source ^ jnp.where(slot >= 2, 1, 0)
        while len(table_refs) == 1 and bits < total // rows:
            source = source ^ jnp.where((slot & bits) != 0, 1, 0)
            bits *= 2
        mine = (spot >= low) & (spot < low + capacity)
        code = jnp.where(mine, source * capacity + spot - low, -1).astype(f32)
        pick = rounded(jnp.where(code == place, 1.0, 0.0))
        blocks = jnp.where(lane < length, part[:, :width], jnp.zeros_like(part[:, :width]))
        samples = dot(pick, blocks)
        if after is not None:
            pick_after = rounded(jnp.where(code == after, 1.0, 0.0))
            samples = samples + dot(pick_after, rounded(dot(part[:, :lanes], shift)))
        return samples

    if total == chunk:
        return part_samples(jnp.concatenate([ref[...] for ref in table_refs], axis=0), 0)
    (table_ref,) = table_refs
    return lax.fori_loop(
        0,
        total // chunk,
        lambda i, s: s + part_samples(table_ref[rows_at(i, chunk), :], i * chunk),
        jnp.zeros((frames, width), f32),
    )


def head_body(rows, length, capacity, place_ref, *refs):
    *table_refs, head_ref = refs
    place = place_ref[0:tail_rows, :]
    head_ref[...] = rounded(assembled(rows, length, capacity, table_refs, place, None, lanes))


def windows(samples, start, per_block, offset):
    inside = iota(samples.shape, 1) - hop * lax.rem(iota((samples.shape[0], 1), 0) + start, per_block)
    inside = inside - offset
    return jnp.where((inside >= 0) & (inside < hop), samples, jnp.zeros_like(samples))


def rows_at(step, count):
    return pl.ds(pl.multiple_of(step * count, count), count)


def zero_forward_body(rows, length, capacity, place_ref, after_ref, ce_ref, co_ref, gains_ref, *refs):
    *table_refs, samples_ref, act_even, act_odd = refs[:-6]
    scaled_even, scaled_odd, slope_even, slope_odd, spread_even, spread_odd = refs[-6:]
    per_block = length // hop
    samples = rounded(
        assembled(
            rows, length, capacity, table_refs, place_ref[...], after_ref[...], samples_ref.shape[1]
        )
    )
    samples_ref[...] = samples
    for conv, offset, act, scaled_ref, slope_ref, spread_ref in (
        (ce_ref, 0, act_even, scaled_even, slope_even, spread_even),
        (co_ref, hop // 2, act_odd, scaled_odd, slope_odd, spread_odd),
    ):
        pre = dot(windows(samples, 0, per_block, offset), conv[...])
        scaled, spread, normed = norm_parts(pre, gains_ref[0:1, :], gains_ref[1:2, :])
        value, slope = gelu_parts(normed)
        act[...] = rounded(value)
        scaled_ref[...] = scaled
        slope_ref[...] = slope
        spread_ref[...] = jnp.broadcast_to(spread, spread_ref.shape)


def layers_body(
    length, split,
    samples_ref, after_ref, ce_ref, co_ref, gains_ref, act_even, act_odd, cotangent_ref, conv_one_ref,
    feats_ref, back_one, back_prev, back_tail, fix_patch, fix_scaled, fix_slope, fix_spread,
    small_ref, *rest,
):
    keep = jnp.where(lax.axis_index("seq") < lax.axis_size("seq") - 1, 1.0, 0.0)
    frames, width = feats_ref.shape
    span = samples_ref.shape[1]
    per_block = length // hop
    if split:
        *split_refs, grad_ref, wide, act_last, act_next = rest
    else:
        grad_ref, wide, act_last, act_next = rest

    last = frames - tail_rows
    row = iota((lanes, span), 0)
    shift = rounded(jnp.where((iota((lanes, span), 1) == row + length) & (row < hop), keep, 0.0))
    after = dot(after_ref[...], shift)[0:1, :]
    patch_last = samples_ref[pl.ds(last, tail_rows), :].astype(f32)
    patch_last = windows(rounded(patch_last + jnp.where(iota((tail_rows, 1), 0) >= tail_rows - 1, after, 0.0)), last, per_block, hop // 2)
    patch_extra = rounded(jnp.where(iota((tail_rows, 1), 0) == 0, after, 0.0))
    fix_patch[0:tail_rows, :] = patch_last
    fix_patch[tail_rows:, :] = patch_extra
    pre = jnp.concatenate([dot(patch_last, co_ref[...]), dot(patch_extra, ce_ref[...])], axis=0)
    scaled, spread, normed = norm_parts(pre, gains_ref[0:1, :], gains_ref[1:2, :])
    value, slope = gelu_parts(normed)
    fix_scaled[...] = scaled
    fix_slope[...] = slope
    fix_spread[...] = jnp.broadcast_to(spread, fix_spread.shape)
    act_last[0:last, :] = act_odd[0:last, :]
    act_last[last:, :] = rounded(value[:tail_rows])
    wide[0:frames, :] = act_even[...].astype(f32)
    wide[pl.ds(frames, 8), :] = value[tail_rows : tail_rows + 8] * keep
    act_next[...] = rounded(wide[pl.ds(1, frames), :])

    wide[0:8, :] = jnp.zeros((8, width), f32)
    gain_sum, bias_sum = 0.0, 0.0
    count = frames // 4
    parts = [pl.ds(k * count, count) for k in range(4)]
    pre_parts = [
        dot(act_even[at, :], conv_one_ref[0:width, :])
        + dot(act_last[at, :], conv_one_ref[width : 2 * width, :])
        + dot(act_next[at, :], conv_one_ref[2 * width :, :])
        for at in parts
    ]
    for k, (at, pre) in enumerate(zip(parts, pre_parts)):
        scaled, spread, normed = norm_parts(pre, gains_ref[2:3, :], gains_ref[3:4, :])
        value, slope = gelu_parts(normed)
        feats_ref[at, :] = rounded(value)
        inner = cotangent_ref[at, :].astype(f32) * slope
        back = norm_back(inner, gains_ref[2:3, :], scaled, spread)
        back_one[at, :] = rounded(back)
        wide[pl.ds(8 + k * count, count), :] = back
        gain_sum = gain_sum + jnp.sum(inner * scaled, axis=0, keepdims=True)
        bias_sum = bias_sum + jnp.sum(inner, axis=0, keepdims=True)
    small_ref[0:1, :] = gain_sum
    small_ref[1:2, :] = bias_sum

    back_prev[...] = rounded(wide[pl.ds(7, frames), :])
    first = iota((tail_rows, 1), 0) == 0
    back_tail[...] = rounded(jnp.where(first, wide[pl.ds(frames + 7, 1), :] * keep, 0.0))
    back = back_one[...]
    grad_ref[0:width, :] = dot_rows(act_even[...], back).astype(grad_ref.dtype)
    grad_ref[width : 2 * width, :] = dot_rows(act_last[...], back).astype(grad_ref.dtype)
    grad_ref[2 * width :, :] = dot_rows(act_next[...], back).astype(grad_ref.dtype)
    if split:
        core, _, _ = chip_bits()
        share = grad_ref.shape[0] // 8
        start = 0
        for side in range(2):
            sent_ref, keep_ref = split_refs[2 * side : 2 * side + 2]
            count = keep_ref.shape[0] // 4
            for k in range(4):
                at = pl.ds(k * count, count)
                for ref, index in ((keep_ref, 2 * k + core), (sent_ref, 2 * k + 1 - core)):
                    ref[at, :] = grad_ref[pl.ds(pl.multiple_of(index * share + start, 16), count), :]
            start += count


def zero_backward_body(
    length,
    samples_ref, fix_patch, conv_one_ref, gains_ref, back_one, back_prev, back_tail,
    scaled_even, scaled_odd, slope_even, slope_odd, spread_even, spread_odd,
    fix_scaled, fix_slope, fix_spread, small_one,
    *rest,
):
    small_ref = rest[0] if len(rest) == 1 else rest[1]
    frames, width = back_one.shape
    span = samples_ref.shape[1]
    per_block = length // hop
    gain = gains_ref[0:1, :]
    last = frames - tail_rows
    back = back_one[...]
    third = conv_one_ref[2 * width :, :]
    up_even = dot_lanes(back, conv_one_ref[0:width, :]) + dot_lanes(back_prev[...], third)
    up_odd = dot_lanes(back, conv_one_ref[width : 2 * width, :])
    up_fix = jnp.concatenate([up_odd[last:], dot_lanes(back_tail[...], third)], axis=0)
    gain_sum, bias_sum, parts = 0.0, 0.0, []
    for up, scaled, slope, spread in (
        (up_even, scaled_even[...], slope_even[...], spread_even[:, 0:1]),
        (up_odd[:last], scaled_odd[0:last, :], slope_odd[0:last, :], spread_odd[0:last, 0:1]),
        (up_fix, fix_scaled[...], fix_slope[...], fix_spread[:, 0:1]),
    ):
        inner = up * slope
        back = norm_back(inner, gain, scaled, spread)
        high = rounded(back)
        parts.append((high, rounded(back - high.astype(f32))))
        gain_sum = gain_sum + jnp.sum(inner * scaled, axis=0, keepdims=True)
        bias_sum = bias_sum + jnp.sum(inner, axis=0, keepdims=True)

    tap = iota((span, lanes), 1)
    place = iota((span, lanes), 0)
    pick_even = rounded(jnp.where(lax.rem(place, hop) == tap, 1.0, 0.0))
    pick_odd = rounded(jnp.where(lax.rem(place + hop // 2, hop) == tap, 1.0, 0.0))
    samples = samples_ref[...]
    taps_even = rounded(dot(windows(samples, 0, per_block, 0), pick_even))
    taps_odd = rounded(dot(windows(samples, 0, per_block, hop // 2), pick_odd))
    taps_last = rounded(dot(fix_patch[0:tail_rows, :], pick_odd))
    taps_extra = rounded(dot(fix_patch[tail_rows:, :], pick_even))
    taps_fix = jnp.concatenate([taps_last, taps_extra], axis=0)
    grad = 0.0
    for taps, pair in zip((taps_even, taps_odd[:last], taps_fix), parts):
        for part in pair:
            grad = grad + dot_rows(taps, part)
    small_ref[...] = jnp.zeros(small_ref.shape, f32)
    small_ref[0:hop, :] = grad[0:hop, :]
    small_ref[hop : hop + 1, :] = gain_sum
    small_ref[hop + 1 : hop + 2, :] = bias_sum
    small_ref[hop + 2 : hop + 4, :] = small_one[0:2, :]
    if len(rest) > 1:
        sent_ref, _, out_ref = rest
        count = sent_ref.shape[0]
        out_ref[0:count, :] = sent_ref[...]
        store_small(out_ref, count, small_ref[...])


def prepare(conv_zero, place, gains, frames, span, per_block):
    width = conv_zero.shape[1]
    vectors = [g[None] for g in gains]
    scratch = [
        pltpu.VMEM(conv_zero.shape, bf16),
        pltpu.VMEM(place.shape, place.dtype),
        *[pltpu.VMEM(v.shape, f32) for v in vectors],
        pltpu.SemaphoreType.DMA((6,)),
    ]
    return call(
        functools.partial(prepare_body, per_block),
        [((span, width), bf16)] * 2 + [((frames, lanes), f32)] * 2 + [((8, width), f32)],
        conv_zero, place, *vectors,
        scratch=scratch,
        spaces=[pltpu.HBM] * 6,
    )


def run_layers(tables, prepared, cotangent, conv_one, rows, length, capacity, split):
    frames, width = cotangent.shape
    span = tables[0].shape[1]
    per_block = length // hop
    whole, half = ((frames, width), f32), ((frames, width), bf16)
    tail = 2 * tail_rows
    conv_even, conv_odd, place_rows, after_rows, gains = prepared
    (head,) = call(
        functools.partial(head_body, rows, length, capacity),
        [((tail_rows, lanes), bf16)],
        place_rows, *tables,
    )
    count = lax.axis_size("seq")
    after = lax.ppermute(head, "seq", [(i + 1, i) for i in range(count - 1)])
    samples, act_even, act_odd, *saved = call(
        functools.partial(zero_forward_body, rows, length, capacity),
        [((frames, span), bf16)] + [half] * 2 + [whole] * 4 + [((frames, lanes), f32)] * 2,
        place_rows, after_rows, conv_even, conv_odd, gains, *tables,
        flops=4 * 10**9,
    )
    outs = [half] * 3 + [
        ((tail_rows, width), bf16),
        ((tail, span), bf16),
        ((tail, width), f32),
        ((tail, width), f32),
        ((tail, lanes), f32),
        ((8, width), f32),
    ]
    grad = (3 * width, width)
    scratch = [
        pltpu.VMEM((frames + 16, width), f32),
        pltpu.VMEM(*half),
        pltpu.VMEM(*half),
    ]
    if split:
        for count in share_parts(3 * width // 8):
            outs += [((4 * count, width), bf16)] * 2
        scratch = [pltpu.VMEM(grad, bf16)] + scratch
    else:
        outs += [(grad, f32)]
    feats, back_one, back_prev, back_tail, fix_patch, *others = call(
        functools.partial(layers_body, length, split),
        outs,
        samples, after, conv_even, conv_odd, gains, act_even, act_odd, cotangent, conv_one,
        scratch=scratch,
        flops=6 * 10**9,
    )
    fix, small_one, grads = others[:3], others[3], others[4:]

    def backward(sent=None):
        outs, more = [((small_rows, width), f32)], []
        if sent is not None:
            outs.append(((sent.shape[0] + 2 * small_rows, sent.shape[1]), bf16))
            more.append(sent)
        return call(
            functools.partial(zero_backward_body, length),
            outs,
            samples, fix_patch, conv_one, gains, back_one, back_prev, back_tail,
            *saved, *fix, small_one, *more,
            flops=4 * 10**9,
        )

    return feats, grads, backward


def share_parts(share):
    left = 32 * (share // 48)
    return left, share - left


def wide_split(small):
    high = rounded(small)
    return high, rounded(small - high.astype(f32))


def store_small(ref, start, small, parts=2):
    for k, part in enumerate(wide_split(small)[:parts]):
        ref[pl.ds(start + k * small_rows, small_rows), :] = part


def add_small(ref, start, small, parts=2):
    for k, part in enumerate(wide_split(small)[:parts]):
        part = part.astype(f32)
        other = ref[pl.ds(start + k * small_rows, small_rows), :].astype(f32)
        total = part + other if k == 0 else total + (part + other)
    return total


def pass_small(got_ref, got_start, small_ref, sent_ref, sent_start, small_out, got=2, sent=2):
    small = add_small(got_ref, got_start, small_ref[...], got)
    small_out[...] = small
    store_small(sent_ref, sent_start, small, sent)


def chip_bits():
    spot = lax.axis_index("dp")
    return spot & 1, (spot >> 1) & 1, (spot >> 2) & 1


def core_body(left, keep_ref, got_ref, *refs):
    _, near, far = chip_bits()
    if left:
        sent_ref, kept_ref = refs
    else:
        small_ref, sent_ref, kept_ref, small_out = refs
    share = keep_ref.shape[0] // 4

    def total(k, mine):
        at = rows_at(2 * mine + k if left else 2 * k + mine, share)
        return keep_ref[at, :].astype(f32) + got_ref[at, :].astype(f32)

    mine = far if left else near
    for k in range(2):
        at = pl.ds(k * share, share)
        sent_ref[at, :] = rounded(total(k, 1 - mine))
        kept_ref[at, :] = total(k, mine)
    if not left:
        pass_small(got_ref, 4 * share, small_ref, sent_ref, 2 * share, small_out)


def chip_body(left, kept_ref, got_ref, *refs):
    _, near, far = chip_bits()
    if left:
        sent_ref, out_ref = refs
    else:
        small_ref, sent_ref, out_ref, small_out = refs
    share = out_ref.shape[0]
    mine = near if left else far

    def total(index):
        at = rows_at(index, share)
        return kept_ref[at, :] + got_ref[at, :].astype(f32)

    sent_ref[0:share, :] = rounded(total(1 - mine))
    out_ref[...] = total(mine)
    if not left:
        pass_small(got_ref, 2 * share, small_ref, sent_ref, share, small_out)


def time_body(left, kept_ref, got_ref, *refs, got):
    if left:
        (sent_ref,) = refs
    else:
        small_ref, sent_ref, small_out = refs
    share = sent_ref.shape[0] - (0 if left else small_rows)
    at = pl.ds(0, share)
    sent_ref[at, :] = rounded(kept_ref[at, :].astype(f32) + got_ref[at, :].astype(f32))
    if not left:
        pass_small(got_ref, share, small_ref, sent_ref, share, small_out, got, 1)


def left_body(kept_ref, got_ref, out_ref):
    out_ref[...] = kept_ref[...].astype(f32) + got_ref[...].astype(f32)


def last_body(left_ref, kr_ref, gr_ref, small_ref, grad_ref, conv_ref, *vector_refs):
    left, right = share_parts(grad_ref.shape[0])
    at = pl.ds(0, right)
    grad_ref[0:left, :] = left_ref[...]
    grad_ref[left:, :] = kr_ref[at, :].astype(f32) + gr_ref[at, :].astype(f32)
    small = add_small(gr_ref, right, small_ref[...], 1)
    conv_ref[...] = small[0:hop]
    for k, ref in enumerate(vector_refs):
        ref[...] = small[hop + k : hop + k + 1]


def copy_body(a_ref, out_ref, token_ref):
    out_ref[...] = a_ref[...]
    token_ref[...] = jnp.zeros(token_ref.shape, f32)


def sum_over_block(feats, grads, backward):
    sent_left, keep_left, sent_right, keep_right = grads
    width = keep_left.shape[1]
    parts = keep_left.shape[0] // 4, keep_right.shape[0] // 4
    kept_small = ((small_rows, width), f32)

    first_step = functools.partial(time_body, got=2)
    later_step = functools.partial(time_body, got=1)

    def kind(count, left, dtype=bf16, tails=0):
        return ((count * parts[0 if left else 1] + small_rows * tails, width), dtype)

    def stage(body, left, count, *args, behind=None):
        along_chips = body in (core_body, chip_body)
        outs = [kind(count, left, tails=0 if left else 2 if along_chips else 1)]
        if along_chips:
            outs.append(kind(count, left, f32))
        if not left:
            outs.append(kept_small)
        run = functools.partial(body, left)
        return call(run, outs, *args, behind=behind, flops=6 * 10**8)

    got_left = swap(sent_left, 1)
    small, sent_right = backward(sent_right)
    got_right = swap(sent_right, 1)
    sl, kl = stage(core_body, True, 2, keep_left, got_left)
    gl = swap(sl, 4)
    sr, kr, small = stage(core_body, False, 2, keep_right, got_right, small, behind=kl)
    gr = swap(sr, 2)
    feats, token = call(copy_body, [(feats.shape, bf16), ((8, lanes), f32)], feats, behind=sr)
    sl, kl = stage(chip_body, True, 1, kl, gl, behind=token)
    gl = swap(sl, 2)
    sr, kr, small = stage(chip_body, False, 1, kr, gr, small, behind=kl)
    gr = swap(sr, 4)
    (sl,) = stage(first_step, True, 1, kl, gl, behind=kr)
    gl = swap_time(sl, 2)
    sr, small = stage(first_step, False, 1, kr, gr, small, behind=sl)
    gr = swap_time(sr, 1)
    (sl,) = stage(later_step, True, 1, sl, gl, behind=sr)
    gl = swap_time(sl, 1)
    sr, small = stage(later_step, False, 1, sr, gr, small, behind=sl)
    gr = swap_time(sr, 2)
    outs = [((sum(parts), width), f32), ((hop, width), f32)] + [((1, width), f32)] * 4
    (left,) = call(left_body, [kind(1, True, f32)], sl, gl, flops=6 * 10**8)
    grad, conv, *vectors = call(last_body, outs, left, sr, gr, small)
    return feats, grad, conv, [v.reshape(-1) for v in vectors]


def on_device(
    audio_blocks,
    send_list,
    place_list,
    cotangent,
    conv_zero,
    conv_one,
    gain_zero,
    bias_zero,
    gain_one,
    bias_one,
):
    n_data, n_time = lax.axis_size("dp"), lax.axis_size("seq")
    blocks = audio_blocks[0]
    rows, length = blocks.shape
    capacity = send_list.shape[2] // n_data
    small_block = n_data == 8 and n_time == 4
    tables = gather_blocks(blocks, send_list[0])
    gains = (gain_zero, bias_zero, gain_one, bias_one)
    prepared = prepare(
        conv_zero, place_list[0], gains, cotangent.shape[1], tables[0].shape[1], length // hop
    )
    feats, grads, backward = run_layers(
        tables, prepared, cotangent[0], conv_one, rows, length, capacity, small_block
    )
    if small_block:
        feats, grad, conv, vectors = sum_over_block(feats, grads, backward)
    else:
        grad = lax.psum_scatter(grads[0], "dp", scatter_dimension=0, tiled=True)
        grad = lax.psum(grad, "seq")
        small = lax.psum(backward()[0], ("dp", "seq"))
        conv, vectors = small[0:hop], [small[hop + k] for k in range(4)]
    return (feats[None], grad, conv, *vectors)


def solution(mesh):
    placed = (
        P("dp", "seq", None),
        P("seq", "dp", None),
        P("seq", "dp", None),
        P("dp", "seq", None),
        P(),
        P(),
        P(),
        P(),
        P(),
        P(),
    )
    return jax.shard_map(
        on_device,
        mesh=mesh,
        in_specs=placed,
        out_specs=(P("dp", "seq", None), P("dp", None), P(), P(), P(), P(), P()),
        check_vma=False,
    )
```

```python
import functools

import jax
import jax.numpy as jnp
from jax import lax
from jax.experimental import pallas as pl
from jax.experimental.pallas import tpu as pltpu
from jax.sharding import PartitionSpec as P

norm_eps = 1e-05
f32 = jnp.float32
bf16 = jnp.bfloat16
tail_rows = 16
small_rows = 16
lanes = 128
hop = 10


def dot(a, b):
    return jnp.dot(a, b, preferred_element_type=f32)


def dot_rows(a, b):
    return lax.dot_general(a, b, (((0,), (0,)), ((), ())), preferred_element_type=f32)


def dot_lanes(a, b):
    return lax.dot_general(a, b, (((1,), (1,)), ((), ())), preferred_element_type=f32)


def iota(shape, dim):
    return lax.broadcasted_iota(jnp.int32, shape, dim)


def rounded(value):
    return value.astype(bf16)


def row_mean(value):
    return jnp.mean(value, axis=-1, keepdims=True)


def norm_parts(pre_act, gain, bias):
    center = pre_act - row_mean(pre_act)
    spread = lax.rsqrt(row_mean(center * center) + norm_eps)
    scaled = center * spread
    return scaled, spread, scaled * gain + bias


def gelu_parts(normed):
    cdf = 0.5 + 0.5 * lax.erf(normed * 0.7071067811865476)
    density = jnp.exp2(normed * normed * -0.7213475204444817) * 0.3989422804014327
    return normed * cdf, cdf + normed * density


def norm_back(inner, gain, scaled, spread):
    pushed = inner * gain
    return spread * (pushed - row_mean(pushed) - scaled * row_mean(pushed * scaled))


def call(body, outs, *args, scratch=(), spaces=None, flops=0, behind=None):
    spaces = spaces or [pltpu.VMEM] * len(args)
    args = [
        pltpu.with_memory_space_constraint(a, pltpu.HBM) if space == pltpu.HBM else a
        for a, space in zip(args, spaces)
    ]
    size = sum(a.size * a.dtype.itemsize for a in args)
    count = len(args)
    run = body
    if behind is not None:
        args, spaces = [*args, behind], [*spaces, pl.ANY]

        def run(*refs):
            body(*refs[:count], *refs[count + 1 :])

    return pl.pallas_call(
        run,
        out_shape=[jax.ShapeDtypeStruct(s, t) for s, t in outs],
        in_specs=[pl.BlockSpec(memory_space=space) for space in spaces],
        out_specs=[pl.BlockSpec(memory_space=pltpu.VMEM)] * len(outs),
        scratch_shapes=list(scratch),
        compiler_params=pltpu.CompilerParams(vmem_limit_bytes=40 << 20),
        cost_estimate=pl.CostEstimate(flops=flops, bytes_accessed=size, transcendentals=0),
    )(*args)


def swap(value, mask):
    count = lax.axis_size("dp")
    return lax.ppermute(value, "dp", [(i, i ^ mask) for i in range(count)])


def swap_time(value, mask):
    count = lax.axis_size("seq")
    return lax.ppermute(value, "seq", [(i, i ^ mask) for i in range(count)])


def packed(blocks, sends, width):
    rows, length = blocks.shape
    slots = sends.shape[1]
    hit = sends == iota((rows, slots), 0)
    spot = jnp.sum(jnp.where(hit, iota((rows, slots), 1).astype(f32), 0.0), axis=1, keepdims=True)
    blocks = jnp.concatenate([blocks.astype(f32), jnp.zeros((rows, width - length), f32)], axis=1)
    return rounded(jnp.where(iota((rows, width), 1) == length, spot, blocks))


def pack_body(blocks_ref, sends_ref, own_ref, blocks_here, sends_here, sems):
    fetch((blocks_ref, sends_ref), (blocks_here, sends_here), sems)
    own_ref[...] = packed(blocks_here[...], sends_here[...], own_ref.shape[1])


def pair_body(own_ref, blocks_ref, sends_ref, out_ref):
    rows, width = own_ref.shape
    out_ref[0:rows, :] = own_ref[...]
    out_ref[rows:, :] = packed(blocks_ref[...], sends_ref[...], width)


def join_body(a_ref, b_ref, out_ref):
    out_ref[...] = jnp.concatenate([a_ref[...], b_ref[...]], axis=0)


def gather_blocks(blocks, sends):
    rows, length = blocks.shape
    width = -(-(length + hop) // lanes) * lanes
    scratch = [
        pltpu.VMEM(blocks.shape, bf16),
        pltpu.VMEM(sends.shape, sends.dtype),
        pltpu.SemaphoreType.DMA((2,)),
    ]
    (table,) = call(
        pack_body, [((rows, width), bf16)], blocks, sends, scratch=scratch, spaces=[pltpu.HBM] * 2
    )
    (table,) = call(
        pair_body, [((2 * rows, width), bf16)], table, swap(blocks, 1), swap(sends, 1)
    )
    count = lax.axis_size("dp")
    if count == 8:
        return [table, *(swap(table, mask) for mask in (3, 5, 7))]
    step = 2
    while step < count:
        got = swap(table, step | 1)
        step *= 2
        (table,) = call(join_body, [((rows * step, width), bf16)], table, got)
    return [table]


def fetch(refs, buffers, sems):
    copies = [pltpu.make_async_copy(r, b, sems.at[k]) for k, (r, b) in enumerate(zip(refs, buffers))]
    for copy in copies:
        copy.start()
    for copy in copies:
        copy.wait()


def prepare_body(
    per_block,
    conv_hbm, place_hbm, *refs,
):
    vectors, (even_ref, odd_ref, place_ref, after_ref, gains_ref) = refs[:4], refs[4:9]
    conv_here, place_here, *vectors_here, sems = refs[9:]
    fetch((conv_hbm, place_hbm, *vectors), (conv_here, place_here, *vectors_here), sems)
    width = even_ref.shape[0]
    taps = conv_here.shape[0]
    conv = conv_here[...]
    for ref, offset in ((even_ref, 0), (odd_ref, hop // 2)):
        spot = iota((width, taps), 0) + offset
        ref[...] = rounded(
            dot(rounded(jnp.where(lax.rem(spot, hop) == iota((width, taps), 1), 1.0, 0.0)), conv)
        )
    frames = place_ref.shape[0]
    rows = place_here.shape[1]
    place = rounded(jnp.broadcast_to(place_here[...].astype(f32), (lanes, rows)))
    block = lax.div(iota((frames, rows), 0), per_block)
    for ref, offset in ((place_ref, 0), (after_ref, 1)):
        wanted = dot_lanes(rounded(jnp.where(block + offset == iota((frames, rows), 1), 1.0, 0.0)), place)
        ref[...] = jnp.where(iota((frames, 1), 0) + offset * per_block < frames, wanted, -2.0)
    gains_ref[...] = jnp.concatenate([v[...] for v in vectors_here] * 2, axis=0)


def assembled(rows, length, capacity, table_refs, place, after, width):
    here = lax.axis_index("dp")
    total = sum(ref.shape[0] for ref in table_refs)
    chunk = min(total, lanes)
    frames = place.shape[0]
    place, low = place[:, :chunk], here * capacity
    mark = rounded(jnp.where(iota((tail_rows, table_refs[0].shape[1]), 1) == length, 1.0, 0.0))
    lane = iota((chunk, width), 1)
    if after is not None:
        after = after[:, :chunk]
        row = iota((lanes, width), 0)
        shift = rounded(jnp.where((iota((lanes, width), 1) == row + length) & (row < hop), 1.0, 0.0))

    def part_samples(part, first):
        spot = dot_lanes(mark, part)[0:1, :].astype(jnp.int32)
        slot = lax.div(iota((1, chunk), 1) + first, rows)
        source, bits = slot ^ here, 2
        if len(table_refs) > 1:
            source = source ^ jnp.where(slot >= 2, 1, 0)
        while len(table_refs) == 1 and bits < total // rows:
            source = source ^ jnp.where((slot & bits) != 0, 1, 0)
            bits *= 2
        mine = (spot >= low) & (spot < low + capacity)
        code = jnp.where(mine, source * capacity + spot - low, -1).astype(f32)
        pick = rounded(jnp.where(code == place, 1.0, 0.0))
        blocks = jnp.where(lane < length, part[:, :width], jnp.zeros_like(part[:, :width]))
        samples = dot(pick, blocks)
        if after is not None:
            pick_after = rounded(jnp.where(code == after, 1.0, 0.0))
            samples = samples + dot(pick_after, rounded(dot(part[:, :lanes], shift)))
        return samples

    if total == chunk:
        return part_samples(jnp.concatenate([ref[...] for ref in table_refs], axis=0), 0)
    (table_ref,) = table_refs
    return lax.fori_loop(
        0,
        total // chunk,
        lambda i, s: s + part_samples(table_ref[rows_at(i, chunk), :], i * chunk),
        jnp.zeros((frames, width), f32),
    )


def head_body(rows, length, capacity, place_ref, *refs):
    *table_refs, head_ref = refs
    place = place_ref[0:tail_rows, :]
    head_ref[...] = rounded(assembled(rows, length, capacity, table_refs, place, None, lanes))


def windows(samples, start, per_block, offset):
    inside = iota(samples.shape, 1) - hop * lax.rem(iota((samples.shape[0], 1), 0) + start, per_block)
    inside = inside - offset
    return jnp.where((inside >= 0) & (inside < hop), samples, jnp.zeros_like(samples))


def rows_at(step, count):
    return pl.ds(pl.multiple_of(step * count, count), count)


def zero_forward_body(rows, length, capacity, place_ref, after_ref, ce_ref, co_ref, gains_ref, *refs):
    *table_refs, samples_ref, act_even, act_odd = refs[:-6]
    scaled_even, scaled_odd, slope_even, slope_odd, spread_even, spread_odd = refs[-6:]
    per_block = length // hop
    samples = rounded(
        assembled(
            rows, length, capacity, table_refs, place_ref[...], after_ref[...], samples_ref.shape[1]
        )
    )
    samples_ref[...] = samples
    for conv, offset, act, scaled_ref, slope_ref, spread_ref in (
        (ce_ref, 0, act_even, scaled_even, slope_even, spread_even),
        (co_ref, hop // 2, act_odd, scaled_odd, slope_odd, spread_odd),
    ):
        pre = dot(windows(samples, 0, per_block, offset), conv[...])
        scaled, spread, normed = norm_parts(pre, gains_ref[0:1, :], gains_ref[1:2, :])
        value, slope = gelu_parts(normed)
        act[...] = rounded(value)
        scaled_ref[...] = scaled
        slope_ref[...] = slope
        spread_ref[...] = jnp.broadcast_to(spread, spread_ref.shape)


def layers_body(
    length, split,
    samples_ref, after_ref, ce_ref, co_ref, gains_ref, act_even, act_odd, cotangent_ref, conv_one_ref,
    feats_ref, back_one, back_prev, back_tail, fix_patch, fix_scaled, fix_slope, fix_spread,
    small_ref, *rest,
):
    keep = jnp.where(lax.axis_index("seq") < lax.axis_size("seq") - 1, 1.0, 0.0)
    frames, width = feats_ref.shape
    span = samples_ref.shape[1]
    per_block = length // hop
    if split:
        *split_refs, grad_ref, wide, act_last, act_next = rest
    else:
        grad_ref, wide, act_last, act_next = rest

    last = frames - tail_rows
    row = iota((lanes, span), 0)
    shift = rounded(jnp.where((iota((lanes, span), 1) == row + length) & (row < hop), keep, 0.0))
    after = dot(after_ref[...], shift)[0:1, :]
    patch_last = samples_ref[pl.ds(last, tail_rows), :].astype(f32)
    patch_last = windows(rounded(patch_last + jnp.where(iota((tail_rows, 1), 0) >= tail_rows - 1, after, 0.0)), last, per_block, hop // 2)
    patch_extra = rounded(jnp.where(iota((tail_rows, 1), 0) == 0, after, 0.0))
    fix_patch[0:tail_rows, :] = patch_last
    fix_patch[tail_rows:, :] = patch_extra
    pre = jnp.concatenate([dot(patch_last, co_ref[...]), dot(patch_extra, ce_ref[...])], axis=0)
    scaled, spread, normed = norm_parts(pre, gains_ref[0:1, :], gains_ref[1:2, :])
    value, slope = gelu_parts(normed)
    fix_scaled[...] = scaled
    fix_slope[...] = slope
    fix_spread[...] = jnp.broadcast_to(spread, fix_spread.shape)
    act_last[0:last, :] = act_odd[0:last, :]
    act_last[last:, :] = rounded(value[:tail_rows])
    wide[0:frames, :] = act_even[...].astype(f32)
    wide[pl.ds(frames, 8), :] = value[tail_rows : tail_rows + 8] * keep
    act_next[...] = rounded(wide[pl.ds(1, frames), :])

    wide[0:8, :] = jnp.zeros((8, width), f32)
    gain_sum, bias_sum = 0.0, 0.0
    count = frames // 4
    parts = [pl.ds(k * count, count) for k in range(4)]
    pre_parts = [
        dot(act_even[at, :], conv_one_ref[0:width, :])
        + dot(act_last[at, :], conv_one_ref[width : 2 * width, :])
        + dot(act_next[at, :], conv_one_ref[2 * width :, :])
        for at in parts
    ]
    for k, (at, pre) in enumerate(zip(parts, pre_parts)):
        scaled, spread, normed = norm_parts(pre, gains_ref[2:3, :], gains_ref[3:4, :])
        value, slope = gelu_parts(normed)
        feats_ref[at, :] = rounded(value)
        inner = cotangent_ref[at, :].astype(f32) * slope
        back = norm_back(inner, gains_ref[2:3, :], scaled, spread)
        back_one[at, :] = rounded(back)
        wide[pl.ds(8 + k * count, count), :] = back
        gain_sum = gain_sum + jnp.sum(inner * scaled, axis=0, keepdims=True)
        bias_sum = bias_sum + jnp.sum(inner, axis=0, keepdims=True)
    small_ref[0:1, :] = gain_sum
    small_ref[1:2, :] = bias_sum

    back_prev[...] = rounded(wide[pl.ds(7, frames), :])
    first = iota((tail_rows, 1), 0) == 0
    back_tail[...] = rounded(jnp.where(first, wide[pl.ds(frames + 7, 1), :] * keep, 0.0))
    back = back_one[...]
    grad_ref[0:width, :] = dot_rows(act_even[...], back).astype(grad_ref.dtype)
    grad_ref[width : 2 * width, :] = dot_rows(act_last[...], back).astype(grad_ref.dtype)
    grad_ref[2 * width :, :] = dot_rows(act_next[...], back).astype(grad_ref.dtype)
    if split:
        core, _, _ = chip_bits()
        share = grad_ref.shape[0] // 8
        start = 0
        for side in range(2):
            sent_ref, keep_ref = split_refs[2 * side : 2 * side + 2]
            count = keep_ref.shape[0] // 4
            for k in range(4):
                at = pl.ds(k * count, count)
                for ref, index in ((keep_ref, 2 * k + core), (sent_ref, 2 * k + 1 - core)):
                    ref[at, :] = grad_ref[pl.ds(pl.multiple_of(index * share + start, 16), count), :]
            start += count


def zero_backward_body(
    length,
    samples_ref, fix_patch, conv_one_ref, gains_ref, back_one, back_prev, back_tail,
    scaled_even, scaled_odd, slope_even, slope_odd, spread_even, spread_odd,
    fix_scaled, fix_slope, fix_spread, small_one,
    *rest,
):
    small_ref = rest[0] if len(rest) == 1 else rest[1]
    frames, width = back_one.shape
    span = samples_ref.shape[1]
    per_block = length // hop
    gain = gains_ref[0:1, :]
    last = frames - tail_rows
    back = back_one[...]
    third = conv_one_ref[2 * width :, :]
    up_even = dot_lanes(back, conv_one_ref[0:width, :]) + dot_lanes(back_prev[...], third)
    up_odd = dot_lanes(back, conv_one_ref[width : 2 * width, :])
    up_fix = jnp.concatenate([up_odd[last:], dot_lanes(back_tail[...], third)], axis=0)
    gain_sum, bias_sum, parts = 0.0, 0.0, []
    for up, scaled, slope, spread in (
        (up_even, scaled_even[...], slope_even[...], spread_even[:, 0:1]),
        (up_odd[:last], scaled_odd[0:last, :], slope_odd[0:last, :], spread_odd[0:last, 0:1]),
        (up_fix, fix_scaled[...], fix_slope[...], fix_spread[:, 0:1]),
    ):
        inner = up * slope
        back = norm_back(inner, gain, scaled, spread)
        high = rounded(back)
        parts.append((high, rounded(back - high.astype(f32))))
        gain_sum = gain_sum + jnp.sum(inner * scaled, axis=0, keepdims=True)
        bias_sum = bias_sum + jnp.sum(inner, axis=0, keepdims=True)

    tap = iota((span, lanes), 1)
    place = iota((span, lanes), 0)
    pick_even = rounded(jnp.where(lax.rem(place, hop) == tap, 1.0, 0.0))
    pick_odd = rounded(jnp.where(lax.rem(place + hop // 2, hop) == tap, 1.0, 0.0))
    samples = samples_ref[...]
    taps_even = rounded(dot(windows(samples, 0, per_block, 0), pick_even))
    taps_odd = rounded(dot(windows(samples, 0, per_block, hop // 2), pick_odd))
    taps_last = rounded(dot(fix_patch[0:tail_rows, :], pick_odd))
    taps_extra = rounded(dot(fix_patch[tail_rows:, :], pick_even))
    taps_fix = jnp.concatenate([taps_last, taps_extra], axis=0)
    taps = jnp.concatenate([taps_even, taps_odd[:last], taps_fix], axis=0)
    grad = dot_rows(
        jnp.concatenate([taps, taps], axis=0),
        jnp.concatenate([pair[k] for k in range(2) for pair in parts], axis=0),
    )
    small_ref[...] = jnp.zeros(small_ref.shape, f32)
    small_ref[0:hop, :] = grad[0:hop, :]
    small_ref[hop : hop + 1, :] = gain_sum
    small_ref[hop + 1 : hop + 2, :] = bias_sum
    small_ref[hop + 2 : hop + 4, :] = small_one[0:2, :]
    if len(rest) > 1:
        sent_ref, _, out_ref = rest
        count = sent_ref.shape[0]
        out_ref[0:count, :] = sent_ref[...]
        store_small(out_ref, count, small_ref[...])


def prepare(conv_zero, place, gains, frames, span, per_block):
    width = conv_zero.shape[1]
    vectors = [g[None] for g in gains]
    scratch = [
        pltpu.VMEM(conv_zero.shape, bf16),
        pltpu.VMEM(place.shape, place.dtype),
        *[pltpu.VMEM(v.shape, f32) for v in vectors],
        pltpu.SemaphoreType.DMA((6,)),
    ]
    return call(
        functools.partial(prepare_body, per_block),
        [((span, width), bf16)] * 2 + [((frames, lanes), f32)] * 2 + [((8, width), f32)],
        conv_zero, place, *vectors,
        scratch=scratch,
        spaces=[pltpu.HBM] * 6,
    )


def run_layers(tables, prepared, cotangent, conv_one, rows, length, capacity, split):
    frames, width = cotangent.shape
    span = tables[0].shape[1]
    per_block = length // hop
    whole, half = ((frames, width), f32), ((frames, width), bf16)
    tail = 2 * tail_rows
    conv_even, conv_odd, place_rows, after_rows, gains = prepared
    (head,) = call(
        functools.partial(head_body, rows, length, capacity),
        [((tail_rows, lanes), bf16)],
        place_rows, *tables,
    )
    count = lax.axis_size("seq")
    after = lax.ppermute(head, "seq", [(i + 1, i) for i in range(count - 1)])
    samples, act_even, act_odd, *saved = call(
        functools.partial(zero_forward_body, rows, length, capacity),
        [((frames, span), bf16)] + [half] * 2 + [whole] * 4 + [((frames, lanes), f32)] * 2,
        place_rows, after_rows, conv_even, conv_odd, gains, *tables,
        flops=4 * 10**9,
    )
    outs = [half] * 3 + [
        ((tail_rows, width), bf16),
        ((tail, span), bf16),
        ((tail, width), f32),
        ((tail, width), f32),
        ((tail, lanes), f32),
        ((8, width), f32),
    ]
    grad = (3 * width, width)
    scratch = [
        pltpu.VMEM((frames + 16, width), f32),
        pltpu.VMEM(*half),
        pltpu.VMEM(*half),
    ]
    if split:
        for count in share_parts(3 * width // 8):
            outs += [((4 * count, width), bf16)] * 2
        scratch = [pltpu.VMEM(grad, bf16)] + scratch
    else:
        outs += [(grad, f32)]
    feats, back_one, back_prev, back_tail, fix_patch, *others = call(
        functools.partial(layers_body, length, split),
        outs,
        samples, after, conv_even, conv_odd, gains, act_even, act_odd, cotangent, conv_one,
        scratch=scratch,
        flops=6 * 10**9,
    )
    fix, small_one, grads = others[:3], others[3], others[4:]

    def backward(sent=None):
        outs, more = [((small_rows, width), f32)], []
        if sent is not None:
            outs.append(((sent.shape[0] + 2 * small_rows, sent.shape[1]), bf16))
            more.append(sent)
        return call(
            functools.partial(zero_backward_body, length),
            outs,
            samples, fix_patch, conv_one, gains, back_one, back_prev, back_tail,
            *saved, *fix, small_one, *more,
            flops=4 * 10**9,
        )

    return feats, grads, backward


def share_parts(share):
    left = 32 * (share // 48)
    return left, share - left


def wide_split(small):
    high = rounded(small)
    return high, rounded(small - high.astype(f32))


def store_small(ref, start, small, parts=2):
    for k, part in enumerate(wide_split(small)[:parts]):
        ref[pl.ds(start + k * small_rows, small_rows), :] = part


def add_small(ref, start, small, parts=2):
    for k, part in enumerate(wide_split(small)[:parts]):
        part = part.astype(f32)
        other = ref[pl.ds(start + k * small_rows, small_rows), :].astype(f32)
        total = part + other if k == 0 else total + (part + other)
    return total


def pass_small(got_ref, got_start, small_ref, sent_ref, sent_start, small_out, got=2, sent=2):
    small = add_small(got_ref, got_start, small_ref[...], got)
    small_out[...] = small
    store_small(sent_ref, sent_start, small, sent)


def chip_bits():
    spot = lax.axis_index("dp")
    return spot & 1, (spot >> 1) & 1, (spot >> 2) & 1


def core_body(left, keep_ref, got_ref, *refs):
    _, near, far = chip_bits()
    if left:
        sent_ref, kept_ref = refs
    else:
        small_ref, sent_ref, kept_ref, small_out = refs
    share = keep_ref.shape[0] // 4

    def total(k, mine):
        at = rows_at(2 * mine + k if left else 2 * k + mine, share)
        return keep_ref[at, :].astype(f32) + got_ref[at, :].astype(f32)

    mine = far if left else near
    for k in range(2):
        at = pl.ds(k * share, share)
        sent_ref[at, :] = rounded(total(k, 1 - mine))
        kept_ref[at, :] = total(k, mine)
    if not left:
        pass_small(got_ref, 4 * share, small_ref, sent_ref, 2 * share, small_out)


def chip_body(left, kept_ref, got_ref, *refs):
    _, near, far = chip_bits()
    if left:
        sent_ref, out_ref = refs
    else:
        small_ref, sent_ref, out_ref, small_out = refs
    share = out_ref.shape[0]
    mine = near if left else far

    def total(index):
        at = rows_at(index, share)
        return kept_ref[at, :] + got_ref[at, :].astype(f32)

    sent_ref[0:share, :] = rounded(total(1 - mine))
    out_ref[...] = total(mine)
    if not left:
        pass_small(got_ref, 2 * share, small_ref, sent_ref, share, small_out)


def time_body(left, kept_ref, got_ref, *refs, got):
    if left:
        (sent_ref,) = refs
    else:
        small_ref, sent_ref, small_out = refs
    share = sent_ref.shape[0] - (0 if left else small_rows)
    at = pl.ds(0, share)
    sent_ref[at, :] = rounded(kept_ref[at, :].astype(f32) + got_ref[at, :].astype(f32))
    if not left:
        pass_small(got_ref, share, small_ref, sent_ref, share, small_out, got, 1)


def left_body(kept_ref, got_ref, out_ref):
    out_ref[...] = kept_ref[...].astype(f32) + got_ref[...].astype(f32)


def last_body(left_ref, kr_ref, gr_ref, small_ref, grad_ref, conv_ref, *vector_refs):
    left, right = share_parts(grad_ref.shape[0])
    at = pl.ds(0, right)
    grad_ref[0:left, :] = left_ref[...]
    grad_ref[left:, :] = kr_ref[at, :].astype(f32) + gr_ref[at, :].astype(f32)
    small = add_small(gr_ref, right, small_ref[...], 1)
    conv_ref[...] = small[0:hop]
    for k, ref in enumerate(vector_refs):
        ref[...] = small[hop + k : hop + k + 1]


def copy_body(a_ref, out_ref, token_ref):
    out_ref[...] = a_ref[...]
    token_ref[...] = jnp.zeros(token_ref.shape, f32)


def sum_over_block(feats, grads, backward):
    sent_left, keep_left, sent_right, keep_right = grads
    width = keep_left.shape[1]
    parts = keep_left.shape[0] // 4, keep_right.shape[0] // 4
    kept_small = ((small_rows, width), f32)

    first_step = functools.partial(time_body, got=2)
    later_step = functools.partial(time_body, got=1)

    def kind(count, left, dtype=bf16, tails=0):
        return ((count * parts[0 if left else 1] + small_rows * tails, width), dtype)

    def stage(body, left, count, *args, behind=None):
        along_chips = body in (core_body, chip_body)
        outs = [kind(count, left, tails=0 if left else 2 if along_chips else 1)]
        if along_chips:
            outs.append(kind(count, left, f32))
        if not left:
            outs.append(kept_small)
        run = functools.partial(body, left)
        return call(run, outs, *args, behind=behind, flops=6 * 10**8)

    got_left = swap(sent_left, 1)
    small, sent_right = backward(sent_right)
    got_right = swap(sent_right, 1)
    sl, kl = stage(core_body, True, 2, keep_left, got_left)
    gl = swap(sl, 4)
    sr, kr, small = stage(core_body, False, 2, keep_right, got_right, small, behind=kl)
    gr = swap(sr, 2)
    feats, token = call(copy_body, [(feats.shape, bf16), ((8, lanes), f32)], feats, behind=sr)
    sl, kl = stage(chip_body, True, 1, kl, gl, behind=token)
    gl = swap(sl, 2)
    sr, kr, small = stage(chip_body, False, 1, kr, gr, small, behind=kl)
    gr = swap(sr, 4)
    (sl,) = stage(first_step, True, 1, kl, gl, behind=kr)
    gl = swap_time(sl, 2)
    sr, small = stage(first_step, False, 1, kr, gr, small, behind=sl)
    gr = swap_time(sr, 1)
    (sl,) = stage(later_step, True, 1, sl, gl, behind=sr)
    gl = swap_time(sl, 1)
    sr, small = stage(later_step, False, 1, sr, gr, small, behind=sl)
    gr = swap_time(sr, 2)
    outs = [((sum(parts), width), f32), ((hop, width), f32)] + [((1, width), f32)] * 4
    (left,) = call(left_body, [kind(1, True, f32)], sl, gl, flops=6 * 10**8)
    grad, conv, *vectors = call(last_body, outs, left, sr, gr, small)
    return feats, grad, conv, [v.reshape(-1) for v in vectors]


def on_device(
    audio_blocks,
    send_list,
    place_list,
    cotangent,
    conv_zero,
    conv_one,
    gain_zero,
    bias_zero,
    gain_one,
    bias_one,
):
    n_data, n_time = lax.axis_size("dp"), lax.axis_size("seq")
    blocks = audio_blocks[0]
    rows, length = blocks.shape
    capacity = send_list.shape[2] // n_data
    small_block = n_data == 8 and n_time == 4
    tables = gather_blocks(blocks, send_list[0])
    gains = (gain_zero, bias_zero, gain_one, bias_one)
    prepared = prepare(
        conv_zero, place_list[0], gains, cotangent.shape[1], tables[0].shape[1], length // hop
    )
    feats, grads, backward = run_layers(
        tables, prepared, cotangent[0], conv_one, rows, length, capacity, small_block
    )
    if small_block:
        feats, grad, conv, vectors = sum_over_block(feats, grads, backward)
    else:
        grad = lax.psum_scatter(grads[0], "dp", scatter_dimension=0, tiled=True)
        grad = lax.psum(grad, "seq")
        small = lax.psum(backward()[0], ("dp", "seq"))
        conv, vectors = small[0:hop], [small[hop + k] for k in range(4)]
    return (feats[None], grad, conv, *vectors)


def solution(mesh):
    placed = (
        P("dp", "seq", None),
        P("seq", "dp", None),
        P("seq", "dp", None),
        P("dp", "seq", None),
        P(),
        P(),
        P(),
        P(),
        P(),
        P(),
    )
    return jax.shard_map(
        on_device,
        mesh=mesh,
        in_specs=placed,
        out_specs=(P("dp", "seq", None), P("dp", None), P(), P(), P(), P(), P()),
        check_vma=False,
    )
```
